128 devices in a mesh: dp: 64 (over x, y, z), mp: 2 (over core).
Axes of the slice: x: 4, y: 4, z: 4, core: 2. Of those that a mesh axis runs over, the one named last changes fastest.
Arguments:
- hidden_in: bfloat16 [8192, 896], P('dp'), may hold values from -6 to 6
- cotangent: bfloat16 [3, 8192, 896], P(None, 'dp'), may hold values from -6 to 6
- lengths: int32 [64, 3], P('dp'), may hold values from 1 to 64, 128 in all within a row
- gains: float32 [4, 896], replicated, may hold values from 0.5 to 1.5
- query_codes: bfloat16 [896, 896], P('dp', 'mp'), may hold values from 0 to 255, as said below
- key_codes: bfloat16 [896, 128], P('dp', 'mp'), may hold values from 0 to 255, as said below
- value_codes: bfloat16 [896, 128], P('dp', 'mp'), may hold values from 0 to 255, as said below
- output_codes: bfloat16 [896, 896], P('mp', 'dp'), may hold values from 0 to 255, as said below
- gate_codes: bfloat16 [896, 4864], P('dp', 'mp'), may hold values from 0 to 255, as said below
- upward_codes: bfloat16 [896, 4864], P('dp', 'mp'), may hold values from 0 to 255, as said below
- down_codes: bfloat16 [4864, 896], P('mp', 'dp'), may hold values from 0 to 255, as said below
- query_scale: float32 [896], P('mp'), as said below
- key_scale: float32 [128], P('mp'), as said below
- value_scale: float32 [128], P('mp'), as said below
- output_scale: float32 [896], replicated, as said below
- gate_scale: float32 [4864], P('mp'), as said below
- upward_scale: float32 [4864], P('mp'), as said below
- down_scale: float32 [896], replicated, as said below
Outputs:
- result: bfloat16 [3, 8192, 896], P(None, 'dp')
- input_grad: bfloat16 [8192, 896], P('dp')
- query_grad: float32 [896, 896], P('dp', 'mp')
- key_grad: float32 [896, 128], P('dp', 'mp')
- value_grad: float32 [896, 128], P('dp', 'mp')
- output_grad: float32 [896, 896], P('mp', 'dp')
- gate_grad: float32 [896, 4864], P('dp', 'mp')
- upward_grad: float32 [896, 4864], P('dp', 'mp')
- down_grad: float32 [4864, 896], P('mp', 'dp')
- query_scale_grad: float32 [896], P('mp')
- key_scale_grad: float32 [128], P('mp')
- value_scale_grad: float32 [128], P('mp')
- output_scale_grad: float32 [896], replicated
- gate_scale_grad: float32 [4864], P('mp')
- upward_scale_grad: float32 [4864], P('mp')
- down_scale_grad: float32 [896], replicated
- gains_grad: float32 [4, 896], replicated
The draws below stay inside these ranges and needn't reach their ends.
Inputs may be any that keep to these rules, and one draw needn't show every extreme that they name: Document lengths of each index of dp; they sum to 128, and the longest is 64. `query_codes`: whole numbers. `key_codes`: whole numbers. `value_codes`: whole numbers. `output_codes`: whole numbers. `gate_codes`: whole numbers. `upward_codes`: whole numbers. `down_codes`: whole numbers. `query_scale`: positive. `key_scale`: positive. `value_scale`: positive. `output_scale`: positive. `gate_scale`: positive. `upward_scale`: positive. `down_scale`: positive.
All inputs are finite; a program needn't handle non-finite values.
Results may differ from the reference program's by a relative error of at most 0.02.
Values may be sent and summed in bfloat16 or wider, within the bound.
A program may use at most 320 MiB of HBM per device.

```python
import math
import jax
import jax.numpy as jnp
import numpy as np
from jax import lax

MODEL_WIDTH = 896
QUERY_HEADS = 14
KEY_VALUE_HEADS = 2
HEAD_WIDTH = 64
FF = 4864
TOK_DEV = 128
DOCS = 3
TOKENS = 8192
N_DP = 64


def weight_code_table(key, count_of_rows, col_count):
    return jax.random.randint(key, (count_of_rows, col_count), 0, 256).astype(jnp.float32).astype(jnp.bfloat16)


def column_scale_rows(key, col_count, fan_in, spread):
    lifted = jax.random.uniform(key, (col_count,), jnp.float32, -spread, spread)
    return jnp.exp(lifted) * fan_in ** (-0.5) / 74.0


def draw_query_codes(key, part):
    key = jax.random.fold_in(key, 11)
    return weight_code_table(key, MODEL_WIDTH, QUERY_HEADS * HEAD_WIDTH)


def draw_key_codes(key, part):
    key = jax.random.fold_in(key, 12)
    return weight_code_table(key, MODEL_WIDTH, KEY_VALUE_HEADS * HEAD_WIDTH)


def draw_value_codes(key, part):
    key = jax.random.fold_in(key, 13)
    return weight_code_table(key, MODEL_WIDTH, KEY_VALUE_HEADS * HEAD_WIDTH)


def draw_output_codes(key, part):
    key = jax.random.fold_in(key, 14)
    return weight_code_table(key, QUERY_HEADS * HEAD_WIDTH, MODEL_WIDTH)


def draw_gate_codes(key, part):
    key = jax.random.fold_in(key, 15)
    return weight_code_table(key, MODEL_WIDTH, FF)


def draw_upward_codes(key, part):
    key = jax.random.fold_in(key, 16)
    return weight_code_table(key, MODEL_WIDTH, FF)


def draw_down_codes(key, part):
    key = jax.random.fold_in(key, 17)
    return weight_code_table(key, FF, MODEL_WIDTH)


def draw_query_scale(key, part):
    key = jax.random.fold_in(key, 21)
    return column_scale_rows(key, QUERY_HEADS * HEAD_WIDTH, MODEL_WIDTH, 0.7)


def draw_key_scale(key, part):
    key = jax.random.fold_in(key, 22)
    return column_scale_rows(key, KEY_VALUE_HEADS * HEAD_WIDTH, MODEL_WIDTH, 0.7)


def draw_value_scale(key, part):
    key = jax.random.fold_in(key, 23)
    return column_scale_rows(key, KEY_VALUE_HEADS * HEAD_WIDTH, MODEL_WIDTH, 0.7)


def draw_output_scale(key, part):
    key = jax.random.fold_in(key, 24)
    return column_scale_rows(key, MODEL_WIDTH, QUERY_HEADS * HEAD_WIDTH, 0.7)


def draw_gate_scale(key, part):
    key = jax.random.fold_in(key, 25)
    return column_scale_rows(key, FF, MODEL_WIDTH, 0.7)


def draw_upward_scale(key, part):
    key = jax.random.fold_in(key, 26)
    return column_scale_rows(key, FF, MODEL_WIDTH, 0.7)


def draw_down_scale(key, part):
    key = jax.random.fold_in(key, 27)
    return column_scale_rows(key, MODEL_WIDTH, FF, 0.7)


def block_scale(key, shape, shards, low, high):
    level, own = 1.0, jax.random.fold_in(key, 6)
    for axis_at, parts in shards:
        heights = jnp.exp(jax.random.uniform(jax.random.fold_in(own, axis_at), (parts,), jnp.float32, low / len(shards), high / len(shards)))
        level = level * jnp.repeat(heights, shape[axis_at] // parts).reshape([-1 if axis == axis_at else 1 for axis in range(len(shape))])
    return level


def split_up(number_of, total, limit, lean):
    loads = [(1 << 20) // math.isqrt(rank ** lean) + 1 for rank in range(2, number_of + 1)]
    surplus, counts = total - limit - (number_of - 1), [1] * (number_of - 1)
    while surplus > 0:
        movable = [i for i in range(number_of - 1) if counts[i] < limit]
        whole, left = sum([loads[i] for i in movable]), surplus
        for i in movable:
            addition = min(limit - counts[i], max(1, left * loads[i] // whole), surplus)
            counts[i] = counts[i] + addition
            surplus = surplus - addition
    return np.array([limit] + counts)


def ragged_sizes(key, amount, total, limit, skew):
    if amount == 2:
        one = jax.random.randint(key, (), max(1, total - limit), min(limit, total - 1) + 1)
        return jnp.stack([one, total - one])
    sizes = jnp.asarray(split_up(amount, total, limit, skew), jnp.int32)
    pairs = (amount - 1) // 2
    giver, sink = sizes[1:1 + 2 * pairs:2], sizes[2:2 + 2 * pairs:2]
    margin = jnp.minimum(giver - 1, limit - sink)
    passed = jax.random.randint(jax.random.fold_in(key, 1), (pairs,), 0, 1 << 20) % (margin + 1)
    sizes = sizes.at[1:1 + 2 * pairs:2].set(giver - passed).at[2:2 + 2 * pairs:2].set(sink + passed)
    return sizes[jax.random.permutation(jax.random.fold_in(key, 2), amount)]


def bell_draw(own_key, dims, scale, bound, shards=(), kind=jnp.bfloat16):
    values = scale * jax.random.normal(own_key, dims, jnp.float32)
    if shards:
        values = values * block_scale(own_key, dims, shards, -0.22, 0.18)
    return jnp.clip(values, -bound, bound).astype(kind)


def setup_inputs(seed: int = 0) -> dict:
    keys = jax.random.split(jax.random.key(seed), 19)
    hidden_in = bell_draw(keys[0], (TOKENS, MODEL_WIDTH), 1.0, 6.0, ((0, 64),))
    cotangent = bell_draw(keys[1], (3, TOKENS, MODEL_WIDTH), 1.0, 6.0, ((1, 64),))
    lengths = jax.vmap(lambda own: ragged_sizes(own, DOCS, TOK_DEV, TOK_DEV // 2, 2))(jax.random.split(keys[2], N_DP)).reshape((N_DP, DOCS)).astype(jnp.int32)
    gains = jnp.clip(1.0 + 0.1 * jax.random.normal(keys[3], (4, MODEL_WIDTH), jnp.float32), 0.5, 1.5)
    query_codes = draw_query_codes(jax.random.fold_in(keys[18], 71), 0)
    key_codes = draw_key_codes(jax.random.fold_in(keys[18], 71), 0)
    value_codes = draw_value_codes(jax.random.fold_in(keys[18], 71), 0)
    output_codes = draw_output_codes(jax.random.fold_in(keys[18], 71), 0)
    gate_codes = draw_gate_codes(jax.random.fold_in(keys[18], 71), 0)
    upward_codes = draw_upward_codes(jax.random.fold_in(keys[18], 71), 0)
    down_codes = draw_down_codes(jax.random.fold_in(keys[18], 71), 0)
    query_scale = draw_query_scale(jax.random.fold_in(keys[18], 71), 0)
    key_scale = draw_key_scale(jax.random.fold_in(keys[18], 71), 0)
    value_scale = draw_value_scale(jax.random.fold_in(keys[18], 71), 0)
    output_scale = draw_output_scale(jax.random.fold_in(keys[18], 71), 0)
    gate_scale = draw_gate_scale(jax.random.fold_in(keys[18], 71), 0)
    upward_scale = draw_upward_scale(jax.random.fold_in(keys[18], 71), 0)
    down_scale = draw_down_scale(jax.random.fold_in(keys[18], 71), 0)
    return dict(hidden_in=hidden_in, cotangent=cotangent, lengths=lengths, gains=gains, query_codes=query_codes, key_codes=key_codes, value_codes=value_codes, output_codes=output_codes, gate_codes=gate_codes, upward_codes=upward_codes, down_codes=down_codes, query_scale=query_scale, key_scale=key_scale, value_scale=value_scale, output_scale=output_scale, gate_scale=gate_scale, upward_scale=upward_scale, down_scale=down_scale)


@jax.custom_vjp
def reduced_cast(v):
    return lax.optimization_barrier(v.astype(jnp.bfloat16)).astype(jnp.float32)

@jax.custom_vjp
def reduced_cast_back(v):
    return v

def low_keep(v):
    return (reduced_cast(v), None)

def low_pass(kept, grad):
    return (grad,)

def back_keep(v):
    return (v, None)

def back_low(kept, grad):
    return (reduced_cast(grad),)
reduced_cast.defvjp(low_keep, low_pass)
reduced_cast_back.defvjp(back_keep, back_low)
EPS = 1e-06
CAP = 50.0
BASE = 10000.0
WIDTHS = (8, 4, 2)
HIGH = lax.Precision.HIGHEST

def code_units(code_set, width_bits):
    bin_size = 2.0 ** (8 - width_bits)
    return bin_size * (jnp.floor(code_set / bin_size) + 0.5 - 2.0 ** (width_bits - 1))

def rms_norm(tensor, gain_row):
    return tensor * lax.rsqrt(lax.optimization_barrier(jnp.mean(tensor * tensor, axis=-1, keepdims=True)) + EPS) * gain_row

def precise_product(left_side, right_side):
    return jnp.dot(left_side, right_side, precision=HIGH, preferred_element_type=jnp.float32)

def doc_tables(lengths, count_of_rows):
    doc_ends = jnp.cumsum(lengths).astype(jnp.int32)
    starts = (doc_ends - lengths).astype(jnp.int32)
    token_ids = jnp.arange(count_of_rows, dtype=jnp.int32)
    segment = lax.optimization_barrier(jnp.sum((token_ids[:, None] >= doc_ends[None, :]).astype(jnp.int32), axis=1)).astype(jnp.int32)
    owners = segment[:, None] == jnp.arange(lengths.shape[0], dtype=jnp.int32)[None, :]
    token_position = (token_ids - lax.optimization_barrier(jnp.sum(jnp.where(owners, starts[None, :], 0), axis=1))).astype(jnp.int32)
    allowed = (segment[:, None] == segment[None, :]) & (token_position[None, :] <= token_position[:, None])
    return (token_position, allowed)

def rotary_apply(tensor, token_position, turning):
    half_size = HEAD_WIDTH // 2
    inv_freq = BASE ** (-2.0 * jnp.arange(half_size, dtype=jnp.float32) / HEAD_WIDTH)
    angles = token_position.astype(jnp.float32)[:, None] * inv_freq[None, :]
    cosine = jnp.cos(angles)[:, None, :]
    sines = turning * jnp.sin(angles)[:, None, :]
    first_half = tensor[..., :half_size]
    second_half = tensor[..., half_size:]
    return jnp.concatenate([first_half * cosine - second_half * sines, second_half * cosine + first_half * sines], axis=-1)

def attend(query_rows, key_rows, value_rows, allowed):
    count_of_rows = key_rows.shape[0]
    grouped_heads = query_rows.reshape(count_of_rows, KEY_VALUE_HEADS, QUERY_HEADS // KEY_VALUE_HEADS, HEAD_WIDTH)
    raw_scores = reduced_cast_back(jnp.einsum('qhgd,khd->hgqk', grouped_heads, key_rows, precision=HIGH) * HEAD_WIDTH ** (-0.5))
    capped = jnp.where(allowed, CAP * jnp.tanh(raw_scores / CAP), -1e+30)
    row_top = lax.optimization_barrier(jnp.max(capped, axis=-1, keepdims=True))
    expos = jnp.exp(capped - row_top)
    prob_rows = reduced_cast(expos / lax.optimization_barrier(jnp.sum(expos, axis=-1, keepdims=True)))
    mixed = jnp.einsum('hgqk,khd->qhgd', prob_rows, value_rows, precision=HIGH)
    return mixed.reshape(count_of_rows, QUERY_HEADS * HEAD_WIDTH)

def layer(hidden_rows, lengths, gains, weight_sets):
    count_of_rows = hidden_rows.shape[0]
    token_position, allowed = doc_tables(lengths, count_of_rows)
    normed_input = reduced_cast(rms_norm(hidden_rows, gains[0]))
    results = []
    for query_weight, key_matrix, value_matrix, output_weight, gate_weight, upward_weight, down_weight in weight_sets:
        query_rows = reduced_cast(rotary_apply(reduced_cast_back(precise_product(normed_input, query_weight)).reshape(count_of_rows, QUERY_HEADS, HEAD_WIDTH), token_position, 1.0))
        key_rows = reduced_cast(rotary_apply(reduced_cast_back(precise_product(normed_input, key_matrix)).reshape(count_of_rows, KEY_VALUE_HEADS, HEAD_WIDTH), token_position, 1.0))
        value_rows = reduced_cast(reduced_cast_back(precise_product(normed_input, value_matrix))).reshape(count_of_rows, KEY_VALUE_HEADS, HEAD_WIDTH)
        mixed = reduced_cast(reduced_cast_back(attend(query_rows, key_rows, value_rows, allowed)))
        branch = reduced_cast_back(precise_product(mixed, output_weight))
        lifted = hidden_rows + rms_norm(branch, gains[1])
        normed_two = reduced_cast(rms_norm(lifted, gains[2]))
        gate_value = reduced_cast_back(precise_product(normed_two, gate_weight))
        upward = reduced_cast_back(precise_product(normed_two, upward_weight))
        activated = reduced_cast(jax.nn.gelu(gate_value, approximate=True) * upward)
        feed = reduced_cast_back(precise_product(activated, down_weight))
        results.append(lifted + rms_norm(feed, gains[3]))
    return jnp.stack(results)

def reference(hidden_in, cotangent, lengths, gains, query_codes, key_codes, value_codes, output_codes, gate_codes, upward_codes, down_codes, query_scale, key_scale, value_scale, output_scale, gate_scale, upward_scale, down_scale):
    code_list = [code_set.astype(jnp.float32) for code_set in (query_codes, key_codes, value_codes, output_codes, gate_codes, upward_codes, down_codes)]
    scale_list = [query_scale, key_scale, value_scale, output_scale, gate_scale, upward_scale, down_scale]
    zero_list = [jnp.zeros(code_set.shape, jnp.float32) for code_set in code_list]

    def forward(inputs, gain_rows, scale_set, zero_set):
        weight_sets = [[reduced_cast(scale_row[None, :] * code_units(code_set, width_bits) + zero_mat) for code_set, scale_row, zero_mat in zip(code_list, scale_set, zero_set)] for width_bits in WIDTHS]
        grouped_rows = inputs.reshape(N_DP, TOK_DEV, MODEL_WIDTH)

        def step_fn(carried, item_pair):
            return (carried, jax.checkpoint(layer)(item_pair[0], item_pair[1], gain_rows, weight_sets))
        _, outputs = lax.scan(step_fn, jnp.zeros((), jnp.float32), (grouped_rows, lengths))
        return jnp.transpose(outputs, (1, 0, 2, 3)).reshape(3, N_DP * TOK_DEV, MODEL_WIDTH)
    inputs = hidden_in.astype(jnp.float32)
    result, pullback = jax.vjp(forward, inputs, gains, scale_list, zero_list)
    grad_in, grad_gains, grad_scales, grad_zeros = pullback(cotangent.astype(jnp.float32))
    return (result.astype(jnp.bfloat16), grad_in.astype(jnp.bfloat16), grad_zeros[0], grad_zeros[1], grad_zeros[2], grad_zeros[3], grad_zeros[4], grad_zeros[5], grad_zeros[6], grad_scales[0], grad_scales[1], grad_scales[2], grad_scales[3], grad_scales[4], grad_scales[5], grad_scales[6], grad_gains)
```

```python
import functools
import math

import jax
import jax.numpy as jnp
from jax import lax
from jax.experimental import pallas as pl
from jax.experimental.pallas import tpu as pltpu
from jax.sharding import PartitionSpec as P
MESH = pl.DeviceIdType.MESH
STRIDE = {"x": 16, "y": 4, "z": 1}
AX = "xyz"
ORDERS = ("zyx", "xzy", "yxz")

class Here:
    def __init__(s):
        s.dp = lax.axis_index("dp"); s.mp = lax.axis_index("mp")
        s.c = {a: lax.rem(s.dp // STRIDE[a], 4) for a in AX}
    def nbr(s, a, d):
        c = s.c[a]
        return (s.dp + (lax.rem(c + d, 4) - c) * STRIDE[a], s.mp)
    def at(s, a, d):
        return lax.rem(s.c[a] + d, 4)

def region(h, buf, slabs, order, phase, v):
    idx = {}
    for i, a in enumerate(order):
        idx[a] = slice(None) if i < phase else (v if i == phase else h.c[a])
    return buf.at[(slabs, idx["x"], idx["y"], idx["z"])]

def rcopy(src, dst, ss, rs, dev):
    return pltpu.make_async_remote_copy(src_ref=src, dst_ref=dst, send_sem=ss, recv_sem=rs, device_id=dev, device_id_type=MESH)

def barrier(h):
    b = pltpu.get_barrier_semaphore()
    for a in AX:
        for d in (1, 3):
            pl.semaphore_signal(b, inc=1, device_id=h.nbr(a, d), device_id_type=MESH)
    pl.semaphore_wait(b, 6)

def ring_A(h, buf, slabs, order, phase, ss, rs):
    a = order[phase]
    r = region(h, buf, slabs, order, phase, h.c[a])
    return [rcopy(r, r, ss.at[0], rs.at[0], h.nbr(a, 1)), rcopy(r, r, ss.at[1], rs.at[1], h.nbr(a, 3))]

def ring_B(h, buf, slabs, order, phase, ss, rs):
    a = order[phase]
    lo, n = slabs.start, slabs.size
    m = n // 2
    r0 = region(h, buf, pl.ds(lo, m), order, phase, h.at(a, 3))
    r1 = region(h, buf, pl.ds(lo + m, n - m), order, phase, h.at(a, 1))
    return [rcopy(r0, r0, ss.at[2], rs.at[2], h.nbr(a, 1)), rcopy(r1, r1, ss.at[3], rs.at[3], h.nbr(a, 3))]

def gather_body(nslab, groups, chunks3, s_ref, out_ref, lsem, ss, rs):
    h = Here()
    me = out_ref.at[:, h.c["x"], h.c["y"], h.c["z"]]
    cp = pltpu.make_async_copy(s_ref, me, lsem); cp.start()
    barrier(h)
    cp.wait()
    sends = []
    for phase in range(3):
        work = []
        for g, (lo, n) in enumerate(groups):
            if phase < 2:
                parts = [(lo, n)]
            else:
                parts = [(lo + a, b) for a, b in chunks3[g]]
            for k, (l, m) in enumerate(parts):
                work.append((g, k, pl.ds(l, m), ss.at[g, phase + k], rs.at[g, phase + k]))
        work.sort(key=lambda w: w[1])
        A = []; B = []
        for g, k, sl, s_, r_ in work:
            A.append(ring_A(h, out_ref, sl, ORDERS[g], phase, s_, r_))
            for c in A[-1]: c.start()
        for i, (g, k, sl, s_, r_) in enumerate(work):
            B.append(ring_B(h, out_ref, sl, ORDERS[g], phase, s_, r_))
            for j in range(2):
                A[i][j].wait_recv(); B[i][j].start()
        for b in B:
            for c in b: c.wait_recv()
        sends += [c for x in A + B for c in x]
    for c in sends: c.wait_send()

def gather(s, groups, chunks3, cid=0, space=pl.ANY):
    nslab = s.shape[0]
    nk = max(len(c) for c in chunks3)
    return pl.pallas_call(
        functools.partial(gather_body, nslab, groups, chunks3),
        out_shape=jax.ShapeDtypeStruct((nslab, 4, 4, 4, 16, 128), s.dtype),
        in_specs=[pl.BlockSpec(memory_space=space)], out_specs=pl.BlockSpec(memory_space=space),
        scratch_shapes=[pltpu.SemaphoreType.DMA, pltpu.SemaphoreType.DMA((3, 2 + nk, 4)), pltpu.SemaphoreType.DMA((3, 2 + nk, 4))],
        compiler_params=pltpu.CompilerParams(collective_id=cid, has_side_effects=True, vmem_limit_bytes=60 << 20),
    )(s)

def barrier9(h):
    b = pltpu.get_barrier_semaphore()
    for a in AX:
        for d in (1, 2, 3):
            pl.semaphore_signal(b, inc=1, device_id=h.nbr(a, d), device_id_type=MESH)
    pl.semaphore_wait(b, 9)

def idx_of(h, order, phase, v):
    idx = {}
    for i, a in enumerate(order):
        idx[a] = slice(None) if i < phase else (v if i == phase else h.c[a])
    return idx["x"], idx["y"], idx["z"]

class Scatter:
    def __init__(s, h, gv, r1, r2, order, phase, lo, n, ss, rs):
        s.__dict__.update(h=h, gv=gv, r1=r1, r2=r2, order=order, phase=phase, lo=lo, n=n)
        a = order[phase]
        s.right, s.left = h.nbr(a, 1), h.nbr(a, 3)
        m = n // 2
        s.h0, s.h1 = (lo, m), (lo + m, n - m)
        R = lambda part, d: gv.at[(pl.ds(*part),) + idx_of(h, order, phase, h.at(a, d))]
        s.first = [rcopy(R(s.h0, 2), r1.at[pl.ds(*s.h0)], ss.at[0], rs.at[0], s.right),
                   rcopy(R(s.h1, 2), r1.at[pl.ds(*s.h1)], ss.at[1], rs.at[1], s.left)]
        s.second = [rcopy(R(s.h1, 1), r2.at[0, pl.ds(*s.h1)], ss.at[2], rs.at[2], s.right),
                    rcopy(R(s.h0, 3), r2.at[1, pl.ds(*s.h0)], ss.at[3], rs.at[3], s.left)]
        s.third = [rcopy(R(s.h0, 1), r2.at[0, pl.ds(*s.h0)], ss.at[4], rs.at[4], s.right),
                   rcopy(R(s.h1, 3), r2.at[1, pl.ds(*s.h1)], ss.at[5], rs.at[5], s.left)]
    def start(s):
        for c in s.first + s.second: c.start()
    def add(s, part, d, srcs):
        ix = idx_of(s.h, s.order, s.phase, s.h.at(s.order[s.phase], d))
        @pl.loop(0, part[1])
        def _(i):
            k = part[0] + i
            t = s.gv[(k,) + ix].astype(jnp.float32)
            for r in srcs: t = t + r[k].astype(jnp.float32)
            s.gv[(k,) + ix] = t.astype(jnp.bfloat16)
    def relay(s):
        s.first[0].wait_recv(); s.add(s.h0, 1, [s.r1]); s.third[0].start()
        s.first[1].wait_recv(); s.add(s.h1, 3, [s.r1]); s.third[1].start()
    def finish(s):
        for c in s.second + s.third: c.wait_recv()
        s.add((s.lo, s.n), 0, [s.r2.at[0], s.r2.at[1]])
    def done(s):
        for c in s.first + s.second + s.third: c.wait_send()

def small_phase(h, a, slots, ss, rs):
    cs = [rcopy(slots.at[h.c[a]], slots.at[h.c[a]], ss.at[d - 1], rs.at[d - 1], h.nbr(a, d)) for d in (1, 2, 3)]
    return cs

def scatter_body(groups, chunks, g_ref, sm_ref, out_ref, smo_ref, gv, r1a, r2a, r1b, r2b, r1c, r2c, slots, lsem, ss, rs, sms, smr):
    h = Here()
    cp = pltpu.make_async_copy(g_ref, gv, lsem); cp.start()
    barrier9(h)
    cp.wait()
    cur = sm_ref[...]
    smc = []
    def small_start(p):
        slots[p, h.c[AX[p]]] = cur
        cs = small_phase(h, AX[p], slots.at[p], sms.at[p], smr.at[p])
        for c in cs: c.start()
        return cs
    def small_end(p, cs):
        for c in cs: c.wait_recv()
        smc.extend(cs)
        return (slots[p, 0] + slots[p, 1]) + (slots[p, 2] + slots[p, 3])
    done = []
    for i, (phase, r1, r2) in enumerate(((2, r1a, r2a), (1, r1b, r2b), (0, r1c, r2c))):
        work = []
        sc = small_start(i)
        for k in range(len(chunks[0]) if phase == 2 else 1):
            for g, (lo, n) in enumerate(groups):
                l, m = (lo + chunks[g][k][0], chunks[g][k][1]) if phase == 2 else (lo, n)
                work.append(Scatter(h, gv, r1, r2, ORDERS[g], phase, l, m, ss.at[g, (2 - phase) if phase < 2 else 3 + k], rs.at[g, (2 - phase) if phase < 2 else 3 + k]))
        for w in work: w.start()
        for w in work: w.relay()
        for w in work: w.finish()
        cur = small_end(i, sc)
        done += work
    smo_ref[...] = cur
    @pl.loop(0, out_ref.shape[0])
    def _(k):
        out_ref[k] = gv[k, h.c["x"], h.c["y"], h.c["z"]].astype(jnp.float32)
    for w in done: w.done()
    for c in smc: c.wait_send()

def scatter(g, sm, groups, chunks, cid=1):
    n = g.shape[0]; nk = max(len(c) for c in chunks)
    bf = jnp.bfloat16; V = pltpu.VMEM
    return pl.pallas_call(
        functools.partial(scatter_body, groups, chunks),
        out_shape=(jax.ShapeDtypeStruct((n, 16, 128), jnp.float32), jax.ShapeDtypeStruct(sm.shape, jnp.float32)),
        in_specs=[pl.BlockSpec(memory_space=pl.ANY), pl.BlockSpec(memory_space=V)],
        out_specs=(pl.BlockSpec(memory_space=V),) * 2,
        scratch_shapes=[V((n, 4, 4, 4, 16, 128), bf), V((n, 4, 4, 16, 128), bf), V((2, n, 4, 4, 16, 128), bf),
                        V((n, 4, 16, 128), bf), V((2, n, 4, 16, 128), bf), V((n, 16, 128), bf), V((2, n, 16, 128), bf),
                        V((3, 4) + sm.shape, jnp.float32),
                        pltpu.SemaphoreType.DMA, pltpu.SemaphoreType.DMA((3, 3 + nk, 6)), pltpu.SemaphoreType.DMA((3, 3 + nk, 6)),
                        pltpu.SemaphoreType.DMA((3, 3)), pltpu.SemaphoreType.DMA((3, 3))],
        compiler_params=pltpu.CompilerParams(collective_id=cid, has_side_effects=True, vmem_limit_bytes=60 << 20),
    )(g, sm)
F32, BF = jnp.float32, jnp.bfloat16
HI = lax.Precision.HIGHEST
MUL = (1.0, 16.0, 64.0)
OFF = (-127.5, -120.0, -96.0)
EPS, CAP = 1e-6, 50.0
GATE, UP, DOWN = 8, 27, 46
C0, C1 = math.sqrt(2 / math.pi), 0.044715

def nn(a, b): return lax.dot_general(a, b, (((1,), (0,)), ((), ())), preferred_element_type=F32)
def nt(a, b): return lax.dot_general(a, b, (((1,), (1,)), ((), ())), preferred_element_type=F32)
def tn(a, b): return lax.dot_general(a, b, (((0,), (0,)), ((), ())), preferred_element_type=F32)
def nt_hi(a, b): return lax.dot_general(a, b, (((1,), (1,)), ((), ())), preferred_element_type=F32, precision=HI)
def nn_hi(a, b): return lax.dot_general(a, b, (((1,), (0,)), ((), ())), preferred_element_type=F32, precision=HI)
def iota(s, d): return lax.broadcasted_iota(jnp.int32, s, d)
def rsum(a): return jnp.sum(a.astype(F32), axis=-1, keepdims=True)
def csum(a): return jnp.sum(a, axis=0, keepdims=True)

def spread_matrix():
    r, c = iota((896, 1024), 0), iota((896, 1024), 1)
    return jnp.where(c == r + 2 * lax.shift_right_logical(r * 4682, 16), 1.0, 0.0)

def units(c, b):
    if b == 0: return c
    return jnp.floor(c * BF(1 / MUL[b]))

def rinv(v): return lax.rsqrt(jnp.sum(v * v, axis=-1, keepdims=True) * (1 / 896) + EPS)
def rms_back(v, r, gain, dy):
    gd = gain * dy
    m = jnp.sum(v * gd, axis=-1, keepdims=True) * (1 / 896)
    return r * gd - v * (r * r * r * m), csum(dy * v * r)

class Comp:
    def __init__(s, **kw): s.__dict__.update(kw)
    def slab(s, k): return s.w[k].reshape(1024, 128)
    def codes(s, lo, n): return jnp.concatenate([s.slab(lo + i) for i in range(n)], axis=1)

    def exchange(s, k, part):
        n = part.shape[0]
        s.xs[k, pl.ds(0, n)] = part.astype(BF)
        c = rcopy(s.xs.at[k, pl.ds(0, n)], s.xr.at[k, pl.ds(0, n)], s.xss.at[k], s.xrs.at[k], (s.h.dp, 1 - s.h.mp))
        c.start(); c.wait()
        return s.xs[k, pl.ds(0, n)].astype(F32) + s.xr[k, pl.ds(0, n)].astype(F32)

    def prologue(s):
        p = spread_matrix()
        s.p[...] = p.astype(BF)
        s.gp[...] = nn_hi(s.gains[...], p)
        s.so[...] = nn_hi(s.o_scale[...], p)
        s.sd[...] = nn_hi(s.d_scale[...], p)
        s.hid[...] = nn(s.hidden[...], s.p[...])
        l0, l1 = s.lengths[0, 0], s.lengths[0, 1]
        def seg_of(i): return jnp.where(i >= l0, 1, 0) + jnp.where(i >= l0 + l1, 1, 0)
        ti, tj = iota((128, 128), 0), iota((128, 128), 1)
        si, sj = seg_of(ti), seg_of(tj)
        s.allow[...] = jnp.where((si == sj) & (tj <= ti), 1.0, 0.0)
        pos = ti - jnp.where(si == 0, 0, jnp.where(si == 1, l0, l0 + l1))
        lane = jnp.bitwise_and(tj, 31).astype(F32)
        ang = pos.astype(F32) * jnp.exp(lane * (-math.log(10000.0) / 32))
        co, si_ = jnp.cos(ang), jnp.sin(ang)
        si_ = jnp.where(jnp.bitwise_and(tj, 63) < 32, -si_, si_)
        s.cos[...] = jnp.concatenate([co] * 4, axis=1)
        s.sin[...] = jnp.concatenate([si_] * 4, axis=1)
        x = s.hid[...]
        nrm = (x * rinv(x) * s.gp[0:1]).astype(BF)
        s.nrm[...] = nrm

    def swap(s, v):
        lane = jnp.bitwise_and(iota((128, 512), 1), 63)
        return jnp.where(lane < 32, pltpu.roll(v, 512 - 32, 1), pltpu.roll(v, 32, 1))

    def attention(s):
        nrm = s.nrm[...]
        rs = rsum(nrm)
        allow = jnp.concatenate([s.allow[...]] * 7, axis=0)
        for b in range(3):
            w = units(s.codes(0, 5), b)
            lin = (nn(nrm, w) * MUL[b] + OFF[b] * rs) * s.qkv_scale[...]
            s.lin[b] = lin
            qk = lin[:, :512]
            qk = (qk * s.cos[...] + s.swap(qk) * s.sin[...]).astype(BF)
            qs = jnp.concatenate([qk[:, 64 * i:64 * i + 64] for i in range(7)], axis=0)
            k = qk[:, 448:512]
            v = lin[:, 512:576].astype(BF)
            s.qs[b], s.k[b], s.v[b] = qs, k, v
            th = jnp.tanh(nt(qs, k) * (0.125 / CAP))
            e = jnp.exp(CAP * th) * allow
            pr = e / jnp.sum(e, axis=-1, keepdims=True)
            s.th[b], s.pr[b] = th, pr
            mx = nn(pr.astype(BF), v).astype(BF)
            mixed = jnp.concatenate([jnp.zeros((128, 64), BF)] + [mx[128 * i:128 * i + 128] for i in range(7)], axis=1)
            s.mixed[pl.ds(128 * b, 128)] = mixed
            wo = units(s.codes(4, 4), b)
            s.acc[pl.ds(128 * b, 128)] = nt(mixed, wo) * MUL[b] + OFF[b] * rsum(mixed)

    def middle(s):
        s.bu[...] = s.exchange(0, s.acc[...])
        for b in range(3):
            d = pl.ds(128 * b, 128)
            br = s.bu[d] * s.so[...]
            lif = s.hid[...] + br * rinv(br) * s.gp[1:2]
            s.lifted[d] = lif
            n2 = (lif * rinv(lif) * s.gp[2:3]).astype(BF)
            s.n2[d] = n2
            s.rsn[d] = jnp.broadcast_to(rsum(n2), (128, 128))
        s.n2t[...] = s.n2[...].T
        s.acc[...] = jnp.zeros_like(s.acc)
        s.asum[...] = jnp.zeros_like(s.asum)

    def srow(s, ref, k, n): return ref[:, pl.ds(pl.multiple_of(k * 128, 128), n * 128)]

    def ffn_fwd(s, k, n):
        wg, wu, wd = s.codes(GATE + k, n), s.codes(UP + k, n), s.codes(DOWN + k, n)
        sg, su = s.srow(s.g_scale, k, n), s.srow(s.u_scale, k, n)
        for b in range(3):
            d = pl.ds(128 * b, 128)
            n2, rs = s.n2[d], s.rsn[d][:, 0:1] * OFF[b]
            g = (nn(n2, units(wg, b)) * MUL[b] + rs) * sg
            u = (nn(n2, units(wu, b)) * MUL[b] + rs) * su
            act = (0.5 * g * (1.0 + jnp.tanh(C0 * (g + C1 * g * g * g))) * u).astype(BF)
            for i in range(n):
                c = slice(128 * i, 128 * i + 128)
                s.g[k + i, d], s.u[k + i, d], s.act[k + i, d] = g[:, c].astype(s.g.dtype), u[:, c].astype(s.g.dtype), act[:, c]
            s.acc[d] += nt(act, units(wd, b)) * MUL[b]
            s.asum[d] += jnp.broadcast_to(rsum(act) * OFF[b], (128, 128))

    def turn(s):
        fu = s.exchange(1, s.acc[...] + s.asum[...][:, 0:1])
        dgain, dsd = 0.0, 0.0
        for b in range(3):
            d = pl.ds(128 * b, 128)
            f = fu[128 * b:128 * b + 128]
            feed = f * s.sd[...]
            r = rinv(feed)
            lif = s.lifted[d]
            res = (lif + feed * r * s.gp[3:4]).astype(BF)
            s.result[b] = nt(res, s.p[...]).astype(BF)
            dy = nn(s.cot[b], s.p[...])
            s.dy[d] = dy.astype(BF)
            df, dg = rms_back(feed, r, s.gp[3:4], dy)
            dgain += dg
            dfl = df.astype(BF)
            dsd += csum(dfl.astype(F32) * f)
            s.dfl[d] = dfl
            dfs = (df * s.sd[...]).astype(BF)
            s.dfs[d] = dfs
            s.rsn[d] = jnp.broadcast_to(rsum(dfs) * OFF[b], (128, 128))
        s.sm[11:12] = dgain
        s.sm[7:8] = dsd
        s.dft[...] = s.dfl[...].T
        s.acc[...] = jnp.zeros_like(s.acc)
        s.asum[...] = jnp.zeros_like(s.asum)

    def ffn_bwd(s, k, n):
        wg, wu, wd = s.codes(GATE + k, n), s.codes(UP + k, n), s.codes(DOWN + k, n)
        sg, su = s.srow(s.g_scale, k, n), s.srow(s.u_scale, k, n)
        gl, ul, al = [], [], []
        gsum, usum = 0.0, 0.0
        get = lambda ref, d: jnp.concatenate([ref[k + i, d] for i in range(n)], axis=1)
        for b in range(3):
            d = pl.ds(128 * b, 128)
            da = nn(s.dfs[d], units(wd, b)) * MUL[b] + s.rsn[d][:, 0:1]
            g, u = get(s.g, d).astype(F32), get(s.u, d).astype(F32)
            t = jnp.tanh(C0 * (g + C1 * g * g * g))
            hp = 0.5 * (1.0 + t)
            du = da * (g * hp)
            dg = da * u * (hp + 0.5 * g * (1.0 - t * t) * C0 * (1.0 + 3 * C1 * g * g))
            dgl, dul = dg.astype(BF), du.astype(BF)
            gl.append(dgl); ul.append(dul); al.append(get(s.act, d))
            gsum += csum(dgl.astype(F32) * g); usum += csum(dul.astype(F32) * u)
            dgs, dus = (dg * sg).astype(BF), (du * su).astype(BF)
            s.acc[d] += (nt(dgs, units(wg, b)) + nt(dus, units(wu, b))) * MUL[b]
            s.asum[d] += jnp.broadcast_to((rsum(dgs) + rsum(dus)) * OFF[b], (128, 128))
        at = lambda ref: ref.at[:, pl.ds(pl.multiple_of(k * 128, 128), n * 128)]
        at(s.gsg)[...] = gsum / sg
        at(s.usg)[...] = usum / su
        gl, ul, al = (jnp.concatenate(t, axis=0) for t in (gl, ul, al))
        for base, lhs, rhs in ((GATE, s.n2t, gl), (UP, s.n2t, ul), (DOWN, s.dft, al)):
            dw = nn(lhs[...], rhs).astype(BF)
            for i in range(n):
                s.dw[base + k + i] = dw[:, 128 * i:128 * i + 128].reshape(s.dw.shape[1:])

    def lower(s):
        valid = jnp.where(jnp.bitwise_and(iota((1, 1024), 1), 15) < 14, 1.0, 0.0)
        dn = s.exchange(2, (s.acc[...] + s.asum[...][:, 0:1]) * valid)
        dg1, dg2, dso, din = 0.0, 0.0, 0.0, 0.0
        for b in range(3):
            d = pl.ds(128 * b, 128)
            lif = s.lifted[d]
            dl, dg = rms_back(lif, rinv(lif), s.gp[2:3], dn[128 * b:128 * b + 128])
            dg2 += dg
            dl = dl + s.dy[d].astype(F32)
            din = din + dl
            bu = s.bu[d]
            br = bu * s.so[...]
            db, dg = rms_back(br, rinv(br), s.gp[1:2], dl)
            dg1 += dg
            dbl = db.astype(BF)
            dso += csum(dbl.astype(F32) * bu)
            s.dbl[d] = dbl
            s.dbs[d] = (db * s.so[...]).astype(BF)
        s.din[...] = din
        s.sm[9:10], s.sm[10:11], s.sm[6:7] = dg1, dg2, dso

    def attention_back(s):
        nsum, dqk, dv, sg = 0.0, 0.0, 0.0, 0.0
        dn = 0.0
        scale = s.qkv_scale[...]
        for b in range(3):
            d = pl.ds(128 * b, 128)
            dbs = s.dbs[d]
            dm = (nn(dbs, units(s.codes(4, 4), b)) * MUL[b] + OFF[b] * rsum(dbs)).astype(BF)
            dms = jnp.concatenate([dm[:, 64 * i + 64:64 * i + 128] for i in range(7)], axis=0)
            th, pr = s.th[b], s.pr[b]
            k, v, qs = s.k[b], s.v[b], s.qs[b]
            dp = nt(dms, v)
            gv = tn(pr.astype(BF), dms)
            dc = pr * (dp - jnp.sum(dp * pr, axis=-1, keepdims=True))
            dr = (dc * (1.0 - th * th)).astype(BF)
            gq = nn(dr, k) * 0.125
            gk = tn(dr, qs) * 0.125
            gqk = jnp.concatenate([gq[128 * i:128 * i + 128] for i in range(7)] + [gk], axis=1)
            gqk = gqk * s.cos[...] - s.swap(gqk) * s.sin[...]
            g = jnp.concatenate([gqk, gv, jnp.zeros((128, 64), F32)], axis=1)
            gl = g.astype(BF)
            gs = (g * scale).astype(BF)
            dn += nt(gs, units(s.codes(0, 5), b)) * MUL[b]
            nsum += rsum(gs) * OFF[b]
            sg += csum(gl.astype(F32) * s.lin[b])
            dqk += gl.astype(F32)
        s.sm[12:13, 0:640] = jnp.where(scale > 0, sg / scale, 0.0)
        valid = jnp.where(jnp.bitwise_and(iota((1, 1024), 1), 15) < 14, 1.0, 0.0)
        nrmt = s.nrm[...].T
        dqk = dqk.astype(BF)
        dw = nn(nrmt, dqk[:, :512]).astype(BF)
        lhs = jnp.concatenate([nrmt, s.dbl[...].T], axis=1)
        rhs = jnp.concatenate([jnp.concatenate([dqk[:, 512:576], jnp.zeros((128, 448), BF)], axis=1), s.mixed[...]], axis=0)
        dw2 = nn(lhs, rhs).astype(BF)
        part = (dn + nsum) * valid
        for i in range(4):
            s.dw[i] = dw[:, 128 * i:128 * i + 128].reshape(s.dw.shape[1:])
            s.dw[4 + i] = dw2[:, 128 * i:128 * i + 128].reshape(s.dw.shape[1:])
        d1 = s.exchange(3, part)
        x = s.hid[...]
        dx, dg = rms_back(x, rinv(x), s.gp[0:1], d1)
        s.sm[8:9] = dg
        s.in_grad[...] = nt((s.din[...] + dx).astype(BF), s.p[...]).astype(BF)

INS = ("hidden", "cot", "lengths", "gains", "qkv_scale", "o_scale", "g_scale", "u_scale", "d_scale")
def comp_scratch(gdt=F32):
    V = pltpu.VMEM
    return dict(
        p=V((896, 1024), BF), gp=V((4, 1024), F32), so=V((1, 1024), F32), sd=V((1, 1024), F32), hid=V((128, 1024), F32),
        allow=V((128, 128), F32), cos=V((128, 512), F32), sin=V((128, 512), F32), nrm=V((128, 1024), BF),
        lin=V((3, 128, 640), F32), qs=V((3, 896, 64), BF), k=V((3, 128, 64), BF), v=V((3, 128, 64), BF),
        th=V((3, 896, 128), F32), pr=V((3, 896, 128), F32), mixed=V((384, 512), BF), acc=V((384, 1024), F32),
        bu=V((384, 1024), F32), lifted=V((384, 1024), F32), n2=V((384, 1024), BF), rsn=V((384, 128), F32), n2t=V((1024, 384), BF),
        asum=V((384, 128), F32), g=V((19, 384, 128), gdt), u=V((19, 384, 128), gdt), act=V((19, 384, 128), BF),
        dy=V((384, 1024), BF), dfl=V((384, 1024), BF), dfs=V((384, 1024), BF), dft=V((1024, 384), BF),
        gsg=V((1, 2432), F32), usg=V((1, 2432), F32), dbl=V((384, 1024), BF), dbs=V((384, 1024), BF), din=V((128, 1024), F32),
        xs=V((4, 384, 1024), BF), xr=V((4, 384, 1024), BF),
        xss=pltpu.SemaphoreType.DMA((4,)), xrs=pltpu.SemaphoreType.DMA((4,)))

def comp_body(names, *refs):
    r = dict(zip(names, refs))
    s = Comp(h=Here(), **r)
    b = pltpu.get_barrier_semaphore()
    pl.semaphore_signal(b, inc=1, device_id=(s.h.dp, 1 - s.h.mp), device_id_type=MESH)
    pl.semaphore_wait(b, 1)
    cp = pltpu.make_async_copy(s.w_in, s.w, s.lsem.at[0]); cp.start()
    s.dw = s.w
    s.sm[...] = jnp.zeros_like(s.sm)
    s.prologue()
    cp.wait()
    s.attention(); s.middle()
    @pl.loop(0, 9)
    def _(j): s.ffn_fwd(2 * j, 2)
    s.ffn_fwd(18, 1)
    s.turn()
    @pl.loop(0, 9)
    def _(j): s.ffn_bwd(2 * j, 2)
    s.ffn_bwd(18, 1)
    s.pack()
    s.lower(); s.attention_back()
    cp = pltpu.make_async_copy(s.w, s.dw_out, s.lsem.at[1]); cp.start(); cp.wait()

def pack(s):
    for i in range(3):
        m = min(1024, 2432 - 1024 * i)
        s.sm[i:i + 1, 0:m] = s.gsg[:, 1024 * i:1024 * i + m]
        s.sm[3 + i:4 + i, 0:m] = s.usg[:, 1024 * i:1024 * i + m]
Comp.pack = pack

def compute(w, ins, cid=2):
    V = pl.BlockSpec(memory_space=pltpu.VMEM)
    A = pl.BlockSpec(memory_space=pl.ANY)
    sc = dict(comp_scratch(), w=pltpu.VMEM((65, 4, 4, 4, 16, 128), BF), lsem=pltpu.SemaphoreType.DMA((2,)))
    names = ("w_in",) + INS + ("dw_out", "result", "in_grad", "sm") + tuple(sc)
    return pl.pallas_call(
        functools.partial(comp_body, names),
        out_shape=(jax.ShapeDtypeStruct((65, 4, 4, 4, 16, 128), BF), jax.ShapeDtypeStruct((3, 128, 896), BF),
                   jax.ShapeDtypeStruct((128, 896), BF), jax.ShapeDtypeStruct((16, 1024), F32)),
        in_specs=[A] + [pl.BlockSpec(memory_space=pltpu.SMEM) if n == "lengths" else V for n in INS],
        out_specs=(A, V, V, V),
        scratch_shapes=list(sc.values()),
        compiler_params=pltpu.CompilerParams(collective_id=cid, has_side_effects=True, vmem_limit_bytes=63 << 20),
    )(w, *ins)
GROUPS = ((0, 22), (22, 22), (44, 21))
CHUNKS = (((0, 22),), ((0, 22),), ((0, 21),))

def local(hidden_in, cotangent, lengths, gains, query_codes, key_codes, value_codes, output_codes, gate_codes, upward_codes, down_codes,
          query_scale, key_scale, value_scale, output_scale, gate_scale, upward_scale, down_scale):
    block = jnp.concatenate([query_codes, key_codes, value_codes, output_codes.T, gate_codes, upward_codes, down_codes.T], axis=1)
    block = jnp.pad(block, ((0, 2), (0, 0))).reshape(16, 65, 128).transpose(1, 0, 2)
    w = gather(block, GROUPS, CHUNKS)
    row = lambda *a: jnp.concatenate(a)[None]
    ins = (hidden_in, cotangent, lengths, gains, row(query_scale, key_scale, value_scale, jnp.zeros((64,), F32)), output_scale[None],
           gate_scale[None], upward_scale[None], down_scale[None])
    dw, result, in_grad, sm = compute(w, ins)
    grads, sm = scatter(dw, sm, GROUPS, CHUNKS)
    g = grads.transpose(1, 0, 2).reshape(16, 65 * 128)[:14]
    p = spread_matrix()
    back = nt_hi(sm, p)
    flat = lambda r: sm[r:r + 3].reshape(3072)[:2432]
    return (result, in_grad, g[:, :448], g[:, 448:512], g[:, 512:576], g[:, 576:1024].T, g[:, 1024:3456], g[:, 3456:5888], g[:, 5888:].T,
            sm[12, :448], sm[12, 448:512], sm[12, 512:576], back[6], flat(0), flat(3), back[7], back[8:12])

def solution(mesh):
    d, c, r = P("dp", None), P("dp", "mp"), P("mp", "dp")
    return jax.shard_map(local, mesh=mesh,
        in_specs=(d, P(None, "dp", None), d, P(), c, c, c, r, c, c, r, P("mp"), P("mp"), P("mp"), P(), P("mp"), P("mp"), P()),
        out_specs=(P(None, "dp", None), d, c, c, c, r, c, c, r, P("mp"), P("mp"), P("mp"), P(), P("mp"), P("mp"), P(), P()),
        check_vma=False)
```

```python
import functools
import math

import jax
import jax.numpy as jnp
from jax import lax
from jax.experimental import pallas as pl
from jax.experimental.pallas import tpu as pltpu
from jax.sharding import PartitionSpec as P
MESH = pl.DeviceIdType.MESH
F32, BF = jnp.float32, jnp.bfloat16
STRIDE = {"x": 16, "y": 4, "z": 1}
AX = "xyz"
ORDERS = ("xzy", "yxz", "zyx")
ATT = ((0, 2), (21, 2), (42, 4))
FFN = (2, 23, 46)
NCH = 9
MUL = (1.0, 16.0, 64.0)
OFF = (-127.5, -120.0, -96.0)
EPS, CAP = 1e-6, 50.0
C0, C1 = math.sqrt(2 / math.pi), 0.044715
W = 896

def nn(a, b): return lax.dot_general(a, b, (((1,), (0,)), ((), ())), preferred_element_type=F32)
def nt(a, b): return lax.dot_general(a, b, (((1,), (1,)), ((), ())), preferred_element_type=F32)
def tn(a, b): return lax.dot_general(a, b, (((0,), (0,)), ((), ())), preferred_element_type=F32)
def iota(s, d): return lax.broadcasted_iota(jnp.int32, s, d)
def rsum(a): return jnp.sum(a.astype(F32), axis=-1, keepdims=True)
def csum(a): return jnp.sum(a, axis=0, keepdims=True)
def units(c, b): return c if b == 0 else jnp.floor(c * BF(1 / MUL[b]))
def rinv(v): return lax.rsqrt(jnp.sum(v * v, axis=-1, keepdims=True) * (1 / W) + EPS)
def rms_back(v, r, gain, dy):
    gd = gain * dy
    m = jnp.sum(v * gd, axis=-1, keepdims=True) * (1 / W)
    return r * gd - v * (r * r * r * m), csum(dy * v * r)
def lanes(a): return jnp.concatenate(a, axis=1)
def rows(a): return jnp.concatenate(a, axis=0)

class Here:
    def __init__(s):
        s.dp = lax.axis_index("dp"); s.mp = lax.axis_index("mp")
        s.c = {a: lax.rem(s.dp // STRIDE[a], 4) for a in AX}
    def nbr(s, a, d):
        c = s.c[a]
        return (s.dp + (lax.rem(c + d, 4) - c) * STRIDE[a], s.mp)
    def at(s, a, d):
        return lax.rem(s.c[a] + d, 4)

def rcopy(src, dst, ss, rs, dev):
    return pltpu.make_async_remote_copy(src_ref=src, dst_ref=dst, send_sem=ss, recv_sem=rs, device_id=dev, device_id_type=MESH)

class Ring:
    def __init__(s, h, reg, axis, lo, n, ss, rs):
        right, left = h.nbr(axis, 1), h.nbr(axis, 3)
        m = n // 2
        r = reg(pl.ds(lo, n), h.c[axis])
        r0 = reg(pl.ds(lo, m), h.at(axis, 3))
        r1 = reg(pl.ds(lo + m, n - m), h.at(axis, 1))
        s.a = [rcopy(r, r, ss.at[0], rs.at[0], right), rcopy(r, r, ss.at[1], rs.at[1], left)]
        s.b = [rcopy(r0, r0, ss.at[2], rs.at[2], right), rcopy(r1, r1, ss.at[3], rs.at[3], left)]
    def start(s):
        for c in s.a: c.start()
    def relay(s):
        for a, b in zip(s.a, s.b):
            a.wait_recv(); b.start()
    def finish(s):
        for c in s.b: c.wait_recv()
    def done(s):
        for c in s.a + s.b: c.wait_send()

class Fold:
    def __init__(s, h, reg, axis, lo, n, r1, r2, ss, rs):
        s.h, s.reg, s.axis, s.lo, s.n, s.r1, s.r2 = h, reg, axis, lo, n, r1, r2
        right, left = h.nbr(axis, 1), h.nbr(axis, 3)
        m = n // 2
        s.h0, s.h1 = (lo, m), (lo + m, n - m)
        R = lambda part, d: reg(pl.ds(*part), h.at(axis, d))
        s.first = [rcopy(R(s.h0, 2), r1.at[pl.ds(*s.h0)], ss.at[0], rs.at[0], right),
                   rcopy(R(s.h1, 2), r1.at[pl.ds(*s.h1)], ss.at[1], rs.at[1], left)]
        s.second = [rcopy(R(s.h1, 1), r2.at[0, pl.ds(*s.h1)], ss.at[2], rs.at[2], right),
                    rcopy(R(s.h0, 3), r2.at[1, pl.ds(*s.h0)], ss.at[3], rs.at[3], left)]
        s.third = [rcopy(R(s.h0, 1), r2.at[0, pl.ds(*s.h0)], ss.at[4], rs.at[4], right),
                   rcopy(R(s.h1, 3), r2.at[1, pl.ds(*s.h1)], ss.at[5], rs.at[5], left)]
    def start(s):
        for c in s.first + s.second: c.start()
    def add(s, part, d):
        v = s.h.at(s.axis, d)
        @pl.loop(0, part[1])
        def _(i):
            k = part[0] + i
            ref = s.reg(k, v)
            ref[...] = (ref[...].astype(F32) + s.r1[k].astype(F32)).astype(BF)
    def relay(s):
        s.first[0].wait_recv(); s.add(s.h0, 1); s.third[0].start()
        s.first[1].wait_recv(); s.add(s.h1, 3); s.third[1].start()
    def total(s, k):
        return s.reg(k, s.h.c[s.axis])[...].astype(F32) + s.r2[0, k].astype(F32) + s.r2[1, k].astype(F32)
    def arrive(s):
        for c in s.second + s.third: c.wait_recv()
    def done(s):
        for c in s.first + s.second + s.third: c.wait_send()

class Layer:
    def __init__(s, **kw): s.__dict__.update(kw)

    def reg3(s, g): return lambda sl, v: s.w.at[sl, v]
    def reg2(s, g): return lambda sl, v: s.pb.at[sl, v]
    def reg1(s, g): return lambda sl, v: s.pb.at[sl, s.h.c[ORDERS[g][1]], v]
    def span(s, g, k):
        if isinstance(k, int):
            return ATT[g] if k < 0 else (FFN[g] + 2 * k, 3 if k == NCH - 1 else 2)
        return FFN[g] + 2 * k, 2
    def ring3(s, k):
        return [Ring(s.h, s.reg3(g), ORDERS[g][2], *s.span(g, k), s.gss.at[g, k + 3], s.grs.at[g, k + 3]) for g in range(3)]
    def all_slabs(s, g): return ATT[g][0], ATT[g][1] + 19
    def compact(s, k):
        for g in range(3):
            lo, n = s.span(g, k)
            c = s.h.c[ORDERS[g][2]]
            for i in range(0, n, 2):
                m = min(2, n - i)
                x = lanes([s.pb[lo + i + j].reshape(256, 128) for j in range(m)])
                y = nn(s.cmat[...], x).astype(BF)
                for j in range(m): s.w[lo + i + j, c] = y[:, 128 * j:128 * j + 128]
    def send3(s, k):
        s.compact(k)
        for r in s.ring3(k): r.start()
    def relay3(s, k):
        for r in s.ring3(k): r.relay()
    def finish3(s, k):
        for r in s.ring3(k): r.finish()
    def done3(s, k):
        for r in s.ring3(k): r.done()

    def fold3(s, k):
        return [Fold(s.h, s.reg3(g), ORDERS[g][2], *s.span(g, k), s.r1a, s.r2a, s.fss.at[g, k + 1], s.frs.at[g, k + 1]) for g in range(3)]
    def fold_start(s, k):
        for f in s.fold3(k): f.start()
    def fold_relay(s, k):
        for f in s.fold3(k): f.relay()
    def fold_expand(s, k):
        for f in s.fold3(k):
            f.arrive()
            for i in range(0, f.n, 2):
                m = min(2, f.n - i)
                x = lanes([f.total(f.lo + i + j).astype(BF) for j in range(m)])
                y = nn(s.emat[...], x).astype(BF)
                for j in range(m): s.pb[f.lo + i + j] = y[:, 128 * j:128 * j + 128].reshape(4, 4, 16, 128)
    def fold_done(s, k):
        for f in s.fold3(k): f.done()
    def fold2(s, part):
        sp = ATT if part else tuple((lo, 19) for lo in FFN)
        return [Fold(s.h, s.reg2(g), ORDERS[g][1], *sp[g], s.r1b, s.r2b, s.fss.at[g, 10 + part], s.frs.at[g, 10 + part]) for g in range(3)]
    def fold1(s, part):
        sp = ATT if part else tuple((lo, 19) for lo in FFN)
        return [Fold(s.h, s.reg1(g), ORDERS[g][0], *sp[g], s.r1c, s.r2c, s.fss.at[g, 12 + part], s.frs.at[g, 12 + part]) for g in range(3)]
    def settle2(s, fs):
        for f in fs:
            f.arrive()
            @pl.loop(0, f.n)
            def _(i): s.pb[f.lo + i, s.h.c[f.axis]] = f.total(f.lo + i).astype(BF)
    def settle1(s, fs):
        for f in fs:
            f.arrive()
            @pl.loop(0, f.n)
            def _(i): s.grads[f.lo + i] = f.total(f.lo + i)

    def small(s, t, p):
        a = AX[p]
        own = s.slots.at[t, p, s.h.c[a]]
        return [rcopy(own, own, s.sss.at[t, p, d - 1], s.srs.at[t, p, d - 1], s.h.nbr(a, d)) for d in (1, 2, 3)]
    def small_start(s, t, p, v):
        s.slots[t, p, s.h.c[AX[p]]] = v
        for c in s.small(t, p): c.start()
    def small_end(s, t, p):
        for c in s.small(t, p): c.wait_recv()
        q = s.slots.at[t, p]
        return (q[0] + q[1]) + (q[2] + q[3])

    def slab(s, k): return s.w[k].reshape(W, 128)
    def codes(s, lo, n): return lanes([s.slab(lo + i) for i in range(n)])
    def exchange(s, k, part):
        n = part.shape[0]
        s.xs[pl.ds(0, n)] = part.astype(BF)
        c = rcopy(s.xs.at[pl.ds(0, n)], s.xr.at[k % 2, pl.ds(0, n)], s.xss.at[k], s.xrs.at[k], (s.h.dp, 1 - s.h.mp))
        c.start(); c.wait()
        return s.xs[pl.ds(0, n)].astype(F32) + s.xr[k % 2, pl.ds(0, n)].astype(F32)

    def matrices(s):
        i, j = iota((224, 256), 0), iota((224, 256), 1)
        s.cmat[...] = jnp.where(j == i + 2 * lax.shift_right_logical(i * 4682, 16), 1.0, 0.0).astype(BF)
        i, j = iota((256, 224), 1), iota((256, 224), 0)
        s.emat[...] = jnp.where(j == i + 2 * lax.shift_right_logical(i * 4682, 16), 1.0, 0.0).astype(BF)

    def prologue(s):
        i = iota((W, 1), 0)
        blk = lax.shift_right_logical(i * 4682, 16)
        r = i - 14 * blk
        c = {"x": lax.shift_right_logical(blk, 4), "y": jnp.bitwise_and(lax.shift_right_logical(blk, 2), 3), "z": jnp.bitwise_and(blk, 3)}
        j = iota((W, W), 1)
        for g in range(2):
            a1, a2, a3 = (c[a] for a in ORDERS[g])
            s.q[g] = jnp.where(j == ((a3 * 4 + a2) * 4 + a1) * 14 + r, 1.0, 0.0).astype(BF)
        l0, l1 = s.lengths[0, 0], s.lengths[0, 1]
        def seg_of(i): return jnp.where(i >= l0, 1, 0) + jnp.where(i >= l0 + l1, 1, 0)
        ti, tj = iota((128, 128), 0), iota((128, 128), 1)
        si, sj = seg_of(ti), seg_of(tj)
        s.allow[...] = jnp.where((si == sj) & (tj <= ti), 1.0, 0.0)
        pos = ti - jnp.where(si == 0, 0, jnp.where(si == 1, l0, l0 + l1))
        lane = jnp.bitwise_and(tj, 31).astype(F32)
        ang = pos.astype(F32) * jnp.exp(lane * (-math.log(10000.0) / 32))
        co, sn = jnp.cos(ang), jnp.sin(ang)
        sn = jnp.where(jnp.bitwise_and(tj, 63) < 32, -sn, sn)
        s.cos[...] = co
        s.sin[...] = sn
        x = s.hidden[...].astype(F32)
        nrm = (x * rinv(x) * s.gains[0:1]).astype(BF)
        s.nrm[2] = nrm
        for g in range(2): s.nrm[g] = nn(nrm, s.q[g]).astype(BF)
        s.qkvs[...] = jnp.zeros_like(s.qkvs)
        s.qkvs[:, 0:576] = lanes([s.q_scale[...], s.k_scale[...], s.v_scale[...]])

    def swap(s, v):
        lane = jnp.bitwise_and(iota((128, 512), 1), 63)
        return jnp.where(lane < 32, pltpu.roll(v, 512 - 32, 1), pltpu.roll(v, 32, 1))

    def probs(s, qs, k):
        th = jnp.tanh(nt(qs, k) * (0.125 / CAP))
        e = jnp.exp(CAP * th) * rows([s.allow[...]] * 7)
        return th, e / jnp.sum(e, axis=-1, keepdims=True)

    def heads(s, qk): return rows([qk[:, 64 * i:64 * i + 64] for i in range(7)]), qk[:, 448:512]

    def attention(s, b):
        rs = rsum(s.nrm[2])
        lin = lanes([nn(s.nrm[0], units(s.codes(0, 2), b)), nn(s.nrm[1], units(s.codes(21, 2), b)), nn(s.nrm[2], units(s.codes(42, 1), b))])
        lin = (lin * MUL[b] + OFF[b] * rs) * s.qkvs[...]
        s.lin[b] = lin.astype(s.lin.dtype)
        qk = lin[:, :512]
        qk = (qk * lanes([s.cos[...]] * 4) + s.swap(qk) * lanes([s.sin[...]] * 4)).astype(BF)
        qs, k = s.heads(qk)
        v = lin[:, 512:576].astype(BF)
        s.qk[b], s.v[b] = qk, v
        _, pr = s.probs(qs, k)
        mx = nn(pr.astype(BF), v).astype(BF)
        mixed = lanes([jnp.zeros((128, 64), BF)] + [mx[128 * i:128 * i + 128] for i in range(7)])
        d = pl.ds(128 * b, 128)
        s.mixed[d] = mixed
        s.acc[0, d] = nt(mixed, units(s.codes(42, 4), b)) * MUL[b] + OFF[b] * rsum(mixed)

    def lifted(s, b):
        br = s.bu[pl.ds(128 * b, 128)] * s.o_scale[...]
        r = rinv(br)
        return s.hidden[...].astype(F32) + br * r * s.gains[1:2], br, r

    def middle(s):
        s.bu[...] = s.exchange(0, s.acc[0])
        for b in range(3):
            d = pl.ds(128 * b, 128)
            lif = s.lifted(b)[0]
            n2 = (lif * rinv(lif) * s.gains[2:3]).astype(BF)
            s.rsn[d] = jnp.broadcast_to(rsum(n2), (128, 128))
            for g in range(2): s.n2[g, d] = nn(n2, s.q[g]).astype(BF)
        for g in range(2): s.n2t[g] = s.n2[g].T
        s.acc[0] = jnp.zeros((384, W), F32)
        s.asum[...] = jnp.zeros_like(s.asum)

    def srow(s, ref, k, n): return ref[:, pl.ds(128 * k if isinstance(k, int) else pl.multiple_of(k * 128, 128), n * 128)]

    def ffn_fwd(s, k, n):
        wg, wu, wd = (s.codes(f + k, n) for f in FFN)
        sg, su = s.srow(s.g_scale, k, n), s.srow(s.u_scale, k, n)
        for b in range(3):
            d = pl.ds(128 * b, 128)
            rs = s.rsn[d][:, 0:1] * OFF[b]
            g = (nn(s.n2[0, d], units(wg, b)) * MUL[b] + rs) * sg
            u = (nn(s.n2[1, d], units(wu, b)) * MUL[b] + rs) * su
            act = (0.5 * g * (1.0 + jnp.tanh(C0 * (g + C1 * g * g * g))) * u).astype(BF)
            for i in range(n):
                c = slice(128 * i, 128 * i + 128)
                s.g[k + i, d], s.u[k + i, d] = g[:, c].astype(BF), u[:, c].astype(BF)
            s.acc[0, d] += nt(act, units(wd, b)) * MUL[b]
            s.asum[0, d] += jnp.broadcast_to(rsum(act) * OFF[b], (128, 128))

    def turn(s):
        fu = s.exchange(1, s.acc[0] + s.asum[0][:, 0:1])
        dgain, dsd = 0.0, 0.0
        for b in range(3):
            d = pl.ds(128 * b, 128)
            f = fu[128 * b:128 * b + 128]
            feed = f * s.d_scale[...]
            r = rinv(feed)
            s.result[b] = (s.lifted(b)[0] + feed * r * s.gains[3:4]).astype(BF)
            df, dg = rms_back(feed, r, s.gains[3:4], s.cot[b].astype(F32))
            dgain += dg
            dfl = df.astype(BF)
            dsd += csum(dfl.astype(F32) * f)
            s.n2[0, d] = dfl
            dfs = (df * s.d_scale[...]).astype(BF)
            s.n2[1, d] = dfs
            s.rsn[d] = jnp.broadcast_to(rsum(dfs) * OFF[b], (128, 128))
        s.sm[11:12] = dgain
        s.sm[7:8] = dsd
        s.dft[...] = s.n2[0].T
        s.acc[...] = jnp.zeros_like(s.acc)
        s.asum[...] = jnp.zeros_like(s.asum)

    def ffn_bwd(s, k, n):
        wg, wu, wd = (s.codes(f + k, n) for f in FFN)
        sg, su = s.srow(s.g_scale, k, n), s.srow(s.u_scale, k, n)
        gl, ul, al = [], [], []
        gsum, usum = 0.0, 0.0
        get = lambda ref, d: lanes([ref[k + i, d] for i in range(n)])
        for b in range(3):
            d = pl.ds(128 * b, 128)
            da = nn(s.n2[1, d], units(wd, b)) * MUL[b] + s.rsn[d][:, 0:1]
            g, u = get(s.g, d).astype(F32), get(s.u, d).astype(F32)
            t = jnp.tanh(C0 * (g + C1 * g * g * g))
            hp = 0.5 * (1.0 + t)
            gelu = g * hp
            du = da * gelu
            dg = da * u * (hp + 0.5 * g * (1.0 - t * t) * C0 * (1.0 + 3 * C1 * g * g))
            dgl, dul = dg.astype(BF), du.astype(BF)
            gl.append(dgl); ul.append(dul); al.append((gelu * u).astype(BF))
            gsum += csum(dgl.astype(F32) * g); usum += csum(dul.astype(F32) * u)
            dgs, dus = (dg * sg).astype(BF), (du * su).astype(BF)
            s.acc[0, d] += nt(dgs, units(wg, b)) * MUL[b]
            s.acc[1, d] += nt(dus, units(wu, b)) * MUL[b]
            s.asum[0, d] += jnp.broadcast_to(rsum(dgs) * OFF[b], (128, 128))
            s.asum[1, d] += jnp.broadcast_to(rsum(dus) * OFF[b], (128, 128))
        at = lambda ref: ref.at[:, pl.ds(128 * k if isinstance(k, int) else pl.multiple_of(k * 128, 128), n * 128)]
        at(s.gsg)[...] = gsum / sg
        at(s.usg)[...] = usum / su
        for base, lhs, rhs in zip(FFN, (s.n2t.at[0], s.n2t.at[1], s.dft), (gl, ul, al)):
            dw = nn(lhs[...], rows(rhs)).astype(BF)
            for i in range(n):
                s.w[base + k + i] = dw[:, 128 * i:128 * i + 128].reshape(4, 224, 128)

    def pack(s):
        for i in range(3):
            m = min(W, 2432 - W * i)
            s.sm[i:i + 1, 0:m] = s.gsg[:, W * i:W * i + m]
            s.sm[3 + i:4 + i, 0:m] = s.usg[:, W * i:W * i + m]

    def lower(s):
        dn = sum(nt((s.acc[g] + s.asum[g][:, 0:1]).astype(BF), s.q[g]) for g in range(2))
        dn = s.exchange(2, dn)
        dg1, dg2, dso, din = 0.0, 0.0, 0.0, 0.0
        for b in range(3):
            d = pl.ds(128 * b, 128)
            lif, br, r = s.lifted(b)
            dl, dg = rms_back(lif, rinv(lif), s.gains[2:3], dn[128 * b:128 * b + 128])
            dg2 += dg
            dl = dl + s.cot[b].astype(F32)
            din = din + dl
            db, dg = rms_back(br, r, s.gains[1:2], dl)
            dg1 += dg
            dbl = db.astype(BF)
            dso += csum(dbl.astype(F32) * s.bu[d])
            s.n2[0, d] = dbl
            s.n2[1, d] = (db * s.o_scale[...]).astype(BF)
        s.din[...] = din
        s.sm[9:10], s.sm[10:11], s.sm[6:7] = dg1, dg2, dso

    def attention_back(s, b):
        d = pl.ds(128 * b, 128)
        dbs = s.n2[1, d]
        dm = (nn(dbs, units(s.codes(42, 4), b)) * MUL[b] + OFF[b] * rsum(dbs)).astype(BF)
        dms = rows([dm[:, 64 * i + 64:64 * i + 128] for i in range(7)])
        v = s.v[b]
        qs, k = s.heads(s.qk[b])
        th, pr = s.probs(qs, k)
        dp = nt(dms, v)
        gv = tn(pr.astype(BF), dms)
        dc = pr * (dp - jnp.sum(dp * pr, axis=-1, keepdims=True))
        dr = (dc * (1.0 - th * th)).astype(BF)
        gq = nn(dr, k) * 0.125
        gk = tn(dr, qs) * 0.125
        gqk = lanes([gq[128 * i:128 * i + 128] for i in range(7)] + [gk])
        gqk = gqk * lanes([s.cos[...]] * 4) - s.swap(gqk) * lanes([s.sin[...]] * 4)
        g = lanes([gqk, gv, jnp.zeros((128, 64), F32)])
        gl = g.astype(BF).astype(F32)
        gs = (g * s.qkvs[...]).astype(BF)
        sg = csum(gl * s.lin[b].astype(F32))
        for i, (c, lo, n) in enumerate(((slice(0, 256), 0, 2), (slice(256, 512), 21, 2), (slice(512, 640), 42, 1))):
            part = nt(gs[:, c], units(s.codes(lo, n), b)) * MUL[b] + rsum(gs[:, c]) * OFF[b]
            e = pl.ds(128 * i, 128)
            if b: s.acc[0, e] += part
            else: s.acc[0, e] = part
        if b:
            s.dqk[...] += gl; s.sqk[...] += sg
        else:
            s.dqk[...] = gl; s.sqk[...] = sg

    def attention_grads(s):
        sc = s.qkvs[...]
        s.sm[12:13, 0:640] = jnp.where(sc > 0, s.sqk[...] / sc, 0.0)
        dqk = s.dqk[...].astype(BF)
        dw = [nn(s.nrm[0].T, dqk[:, 0:256]), nn(s.nrm[1].T, dqk[:, 256:512])]
        lhs = lanes([s.nrm[2].T, s.n2[0].T])
        rhs = rows([lanes([dqk[:, 512:576], jnp.zeros((128, 448), BF)]), s.mixed[...]])
        dw.append(nn(lhs, rhs))
        for (lo, n), x in zip(ATT, dw):
            x = x.astype(BF)
            for i in range(n): s.w[lo + i] = x[:, 128 * i:128 * i + 128].reshape(4, 224, 128)

    def last(s):
        dn = sum(nt(s.acc[0, pl.ds(128 * g, 128)].astype(BF), s.q[g]) for g in range(2)) + s.acc[0, pl.ds(256, 128)]
        dn = s.exchange(3, dn)
        x = s.hidden[...].astype(F32)
        dx, dg = rms_back(x, rinv(x), s.gains[0:1], dn)
        s.sm[8:9] = dg
        s.in_grad[...] = (s.din[...] + dx).astype(BF)

INS = ("block", "hidden", "cot", "lengths", "gains", "q_scale", "k_scale", "v_scale", "o_scale", "g_scale", "u_scale", "d_scale")
OUTS = ("grads", "smo", "result", "in_grad")
def scratch():
    V, D = pltpu.VMEM, pltpu.SemaphoreType.DMA
    return dict(
        w=V((65, 4, 224, 128), BF), pb=V((65, 4, 4, 16, 128), BF),
        r1a=V((65, 224, 128), BF), r2a=V((2, 65, 224, 128), BF), r1b=V((65, 4, 16, 128), BF), r2b=V((2, 65, 4, 16, 128), BF),
        r1c=V((65, 16, 128), BF), r2c=V((2, 65, 16, 128), BF), slots=V((2, 3, 4, 8, W), F32), sm=V((16, W), F32),
        cmat=V((224, 256), BF), emat=V((256, 224), BF), q=V((2, W, W), BF), allow=V((128, 128), F32), cos=V((128, 128), F32),
        sin=V((128, 128), F32), nrm=V((3, 128, W), BF), qkvs=V((1, 640), F32), lin=V((3, 128, 640), BF), qk=V((3, 128, 512), BF),
        v=V((3, 128, 64), BF), mixed=V((384, 512), BF), acc=V((2, 384, W), F32), bu=V((384, W), F32),
        n2=V((2, 384, W), BF), n2t=V((2, W, 384), BF), rsn=V((384, 128), F32), asum=V((2, 384, 128), F32),
        g=V((19, 384, 128), BF), u=V((19, 384, 128), BF), dft=V((W, 384), BF),
        gsg=V((1, 2432), F32), usg=V((1, 2432), F32), din=V((128, W), F32), dqk=V((128, 640), F32),
        sqk=V((1, 640), F32), xs=V((384, W), BF), xr=V((2, 384, W), BF), xss=D((4,)), xrs=D((4,)),
        gss=D((3, 12, 4)), grs=D((3, 12, 4)), fss=D((3, 14, 6)), frs=D((3, 14, 6)), sss=D((2, 3, 3)), srs=D((2, 3, 3)), lsem=D((3,)))

def body(names, *refs):
    h = Here()
    s = Layer(h=h, **dict(zip(names, refs)))
    local = []
    for g in range(3):
        lo, n = s.all_slabs(g)
        a1, a2, _ = ORDERS[g]
        local.append(pltpu.make_async_copy(s.block.at[pl.ds(lo, n)], s.pb.at[pl.ds(lo, n), h.c[a2], h.c[a1]], s.lsem.at[g]))
    for c in local: c.start()
    bar = pltpu.get_barrier_semaphore()
    for a in AX:
        for d in (1, 2, 3):
            pl.semaphore_signal(bar, inc=1, device_id=h.nbr(a, d), device_id_type=MESH)
    pl.semaphore_signal(bar, inc=1, device_id=(h.dp, 1 - h.mp), device_id_type=MESH)
    pl.semaphore_wait(bar, 10)
    for c in local: c.wait()
    one = [Ring(h, s.reg1(g), ORDERS[g][0], *s.all_slabs(g), s.gss.at[g, 0], s.grs.at[g, 0]) for g in range(3)]
    two = [Ring(h, s.reg2(g), ORDERS[g][1], *s.all_slabs(g), s.gss.at[g, 1], s.grs.at[g, 1]) for g in range(3)]
    for r in one: r.start()
    s.matrices()
    for r in one: r.relay()
    s.sm[...] = jnp.zeros_like(s.sm)
    for r in one: r.finish()
    for r in two: r.start()
    s.prologue()
    for r in two: r.relay()
    for r in two: r.finish()
    s.send3(-1); s.send3(0); s.send3(1)
    s.relay3(-1)
    s.send3(2)
    s.finish3(-1)
    s.attention(0)
    s.relay3(0); s.send3(3)
    s.attention(1)
    s.relay3(1); s.send3(4)
    s.attention(2)
    s.relay3(2); s.send3(5)
    s.middle()
    @pl.loop(0, NCH - 1)
    def _(j):
        @pl.when(j < 5)
        def _(): s.relay3(j + 3)
        @pl.when(j == 5)
        def _(): s.relay3(NCH - 1)
        @pl.when(j < 2)
        def _(): s.send3(j + 6)
        @pl.when(j == 2)
        def _(): s.send3(NCH - 1)
        s.finish3(j)
        s.ffn_fwd(2 * j, 2)
    s.finish3(NCH - 1)
    s.ffn_fwd(16, 3)
    s.turn()
    for r in one + two: r.done()
    s.done3(-1); s.done3(NCH - 1)
    @pl.loop(0, NCH - 1)
    def _(j): s.done3(j)
    @pl.loop(0, NCH - 1)
    def _(j):
        s.ffn_bwd(2 * j, 2)
        s.fold_start(j)
        @pl.when(j >= 2)
        def _(): s.fold_relay(j - 2)
    s.ffn_bwd(16, 3)
    s.fold_start(NCH - 1)
    s.fold_relay(NCH - 3)
    s.pack()
    s.lower()
    s.small_start(0, 0, s.sm[0:8])
    s.fold_relay(NCH - 2)
    s.attention_back(0)
    s.fold_relay(NCH - 1)
    @pl.loop(0, 3)
    def _(j): s.fold_expand(j)
    s.attention_back(1)
    @pl.loop(3, 6)
    def _(j): s.fold_expand(j)
    s.small_start(0, 1, s.small_end(0, 0))
    s.attention_back(2)
    s.attention_grads()
    s.fold_start(-1)
    @pl.loop(6, NCH - 1)
    def _(j): s.fold_expand(j)
    s.fold_expand(NCH - 1)
    b_ffn, b_att, c_ffn, c_att = s.fold2(0), s.fold2(1), s.fold1(0), s.fold1(1)
    for f in b_ffn: f.start()
    s.last()
    s.small_start(1, 0, s.sm[8:16])
    s.small_start(0, 2, s.small_end(0, 1))
    s.fold_relay(-1)
    for f in b_ffn: f.relay()
    s.fold_expand(-1)
    for f in b_att: f.start()
    s.settle2(b_ffn)
    for f in c_ffn: f.start()
    s.small_start(1, 1, s.small_end(1, 0))
    for f in b_att: f.relay()
    for f in c_ffn: f.relay()
    s.settle2(b_att)
    for f in c_att: f.start()
    s.small_start(1, 2, s.small_end(1, 1))
    s.settle1(c_ffn)
    for f in c_att: f.relay()
    s.smo[0:8] = s.small_end(0, 2)
    s.settle1(c_att)
    s.smo[8:16] = s.small_end(1, 2)
    s.fold_done(-1); s.fold_done(NCH - 1)
    @pl.loop(0, NCH - 1)
    def _(j): s.fold_done(j)
    for f in b_ffn + b_att + c_ffn + c_att: f.done()
    for t in range(2):
        for p in range(3):
            for c in s.small(t, p): c.wait_send()

def layer(*ins):
    V = pl.BlockSpec(memory_space=pltpu.VMEM)
    sc = scratch()
    sp = [pl.BlockSpec(memory_space=pltpu.SMEM) if n == "lengths" else pl.BlockSpec(memory_space=pl.ANY) if n == "block" else V for n in INS]
    return pl.pallas_call(
        functools.partial(body, INS + OUTS + tuple(sc)),
        out_shape=(jax.ShapeDtypeStruct((65, 16, 128), F32), jax.ShapeDtypeStruct((16, W), F32), jax.ShapeDtypeStruct((3, 128, W), BF),
                   jax.ShapeDtypeStruct((128, W), BF)),
        in_specs=sp, out_specs=(V,) * 4, scratch_shapes=list(sc.values()),
        compiler_params=pltpu.CompilerParams(collective_id=0, has_side_effects=True, vmem_limit_bytes=63 << 20),
    )(*ins)

def unpack_body(g_ref, sm_ref, q, k, v, o, gate, up, down, qs, ks, vs, os, gs, us, ds, gains):
    cat = lambda *spans: lanes([g_ref[i] for lo, n in spans for i in range(lo, lo + n)])
    qk = cat(ATT[0], ATT[1])
    q[...] = qk[:14, :448]
    k[...] = qk[:14, 448:512]
    vo = cat(ATT[2])
    v[...] = vo[:14, :64]
    o[...] = vo.T[64:512, :14]
    gate[...] = cat((FFN[0], 19))[:14]
    up[...] = cat((FFN[1], 19))[:14]
    down[...] = cat((FFN[2], 19)).T[:, :14]
    long = lambda r: lanes([sm_ref[r:r + 1], sm_ref[r + 1:r + 2], sm_ref[r + 2:r + 3, 0:640]])
    gs[...], us[...] = long(0), long(3)
    os[...], ds[...] = sm_ref[6:7], sm_ref[7:8]
    qs[...], ks[...], vs[...] = sm_ref[12:13, 0:448], sm_ref[12:13, 448:512], sm_ref[12:13, 512:576]
    gains[...] = sm_ref[8:12]

def unpack(g, sm):
    shapes = [(14, 448), (14, 64), (14, 64), (448, 14), (14, 2432), (14, 2432), (2432, 14), (1, 448), (1, 64), (1, 64), (1, 896), (1, 2432),
              (1, 2432), (1, 896), (4, 896)]
    V = pl.BlockSpec(memory_space=pltpu.VMEM)
    return pl.pallas_call(unpack_body, out_shape=[jax.ShapeDtypeStruct(x, F32) for x in shapes], in_specs=[V, V], out_specs=[V] * len(shapes),
                          compiler_params=pltpu.CompilerParams(vmem_limit_bytes=32 << 20))(g, sm)

def local(hidden_in, cotangent, lengths, gains, query_codes, key_codes, value_codes, output_codes, gate_codes, upward_codes, down_codes,
          query_scale, key_scale, value_scale, output_scale, gate_scale, upward_scale, down_scale):
    block = jnp.concatenate([query_codes[:, :256], gate_codes, query_codes[:, 256:], key_codes, upward_codes, value_codes, output_codes.T, down_codes.T], axis=1)
    block = jnp.pad(block, ((0, 2), (0, 0))).reshape(16, 65, 128).transpose(1, 0, 2)
    scales = [a[None] for a in (query_scale, key_scale, value_scale, output_scale, gate_scale, upward_scale, down_scale)]
    grads, sm, result, in_grad = layer(block, hidden_in, cotangent, lengths, gains, *scales)
    out = unpack(grads, sm)
    return (result, in_grad, *out[:7], *(a[0] for a in out[7:14]), out[14])

def solution(mesh):
    d, c, r = P("dp", None), P("dp", "mp"), P("mp", "dp")
    return jax.shard_map(local, mesh=mesh,
        in_specs=(d, P(None, "dp", None), d, P(), c, c, c, r, c, c, r, P("mp"), P("mp"), P("mp"), P(), P("mp"), P("mp"), P()),
        out_specs=(P(None, "dp", None), d, c, c, c, r, c, c, r, P("mp"), P("mp"), P("mp"), P(), P("mp"), P("mp"), P(), P()),
        check_vma=False)
```

```python
import functools
import math

import jax
import jax.numpy as jnp
from jax import lax
from jax.experimental import pallas as pl
from jax.experimental.pallas import tpu as pltpu
from jax.sharding import PartitionSpec as P
MESH = pl.DeviceIdType.MESH
F32, BF = jnp.float32, jnp.bfloat16
STRIDE = {"x": 16, "y": 4, "z": 1}
AX = "xyz"
ORDERS = ("xzy", "yxz", "zyx")
ATT = ((0, 2), (2, 2), (4, 4))
FFN = (8, 27, 46)
GATHER_WAVES = ((0, 7), (7, 12))
SUM_WAVES = ((0, 9), (9, 10))
NCH = 10
MUL = (1.0, 16.0, 64.0)
OFF = (-127.5, -120.0, -96.0)
EPS, CAP = 1e-6, 50.0
C0, C1 = math.sqrt(2 / math.pi), 0.044715
W = 896

def nn(a, b): return lax.dot_general(a, b, (((1,), (0,)), ((), ())), preferred_element_type=F32)
def nt(a, b): return lax.dot_general(a, b, (((1,), (1,)), ((), ())), preferred_element_type=F32)
def tn(a, b): return lax.dot_general(a, b, (((0,), (0,)), ((), ())), preferred_element_type=F32)
def iota(s, d): return lax.broadcasted_iota(jnp.int32, s, d)
def rsum(a): return jnp.sum(a.astype(F32), axis=-1, keepdims=True)
def csum(a): return jnp.sum(a, axis=0, keepdims=True)
def units(c, b): return c if b == 0 else jnp.floor(c * BF(1 / MUL[b]))
def rinv(v): return lax.rsqrt(jnp.sum(v * v, axis=-1, keepdims=True) * (1 / W) + EPS)
def rms_back(v, r, gain, dy):
    gd = gain * dy
    m = jnp.sum(v * gd, axis=-1, keepdims=True) * (1 / W)
    return r * gd - v * (r * r * r * m), csum(dy * v * r)
def lanes(a): return jnp.concatenate(a, axis=1)
def rows(a): return jnp.concatenate(a, axis=0)

class Here:
    def __init__(s):
        s.dp = lax.axis_index("dp"); s.mp = lax.axis_index("mp")
        s.c = {a: lax.rem(s.dp // STRIDE[a], 4) for a in AX}
    def nbr(s, a, d):
        c = s.c[a]
        return (s.dp + (lax.rem(c + d, 4) - c) * STRIDE[a], s.mp)
    def at(s, a, d):
        return lax.rem(s.c[a] + d, 4)

def rcopy(src, dst, ss, rs, dev):
    return pltpu.make_async_remote_copy(src_ref=src, dst_ref=dst, send_sem=ss, recv_sem=rs, device_id=dev, device_id_type=MESH)

def halves(lo, n):
    if n == 1: return (lo, 1, 0), (lo, 1, 1)
    return (lo, n // 2, None), (lo + n // 2, n - n // 2, None)
def cut(ref, part): return ref if part[2] is None else ref.at[:, pl.ds(112 * part[2], 112)]

def take_bytes(ref, sem, h):
    rcopy(ref, ref, sem, sem, (h.dp, 1 - h.mp)).wait_recv()

class Rings:
    def __init__(s, h, regs, phase, spans, ss, rs, size):
        s.h, s.ss, s.rs, s.size, s.n = h, ss, rs, size, sum(n for _, n in spans)
        s.a, s.b = [], []
        for g, (lo, n) in enumerate(spans):
            axis, reg = ORDERS[g][phase], regs[g]
            right, left = h.nbr(axis, 1), h.nbr(axis, 3)
            p0, p1 = halves(lo, n)
            r = reg(pl.ds(lo, n), h.c[axis])
            r0 = cut(reg(pl.ds(*p0[:2]), h.at(axis, 3)), p0)
            r1 = cut(reg(pl.ds(*p1[:2]), h.at(axis, 1)), p1)
            s.a += [rcopy(r, r, ss, rs.at[0], right), rcopy(r, r, ss, rs.at[0], left)]
            s.b += [rcopy(r0, r0, ss, rs.at[1], right), rcopy(r1, r1, ss, rs.at[1], left)]
    def start(s):
        for c in s.a: c.start()
    def relay(s):
        take_bytes(s.size(2, s.n), s.rs.at[0], s.h)
        for c in s.b: c.start()
    def finish(s):
        take_bytes(s.size(1, s.n), s.rs.at[1], s.h)

class Folds:
    def __init__(s, h, regs, phase, spans, r1, r2, ss, rs, take, size):
        s.h, s.ss, s.rs, s.size, s.n = h, ss, rs, size, sum(n for _, n in spans)
        s.r1, s.r2, s.take = r1, r2, take
        s.first, s.second, s.third, s.parts, s.items = [], [], [], [], []
        l, r = r2.at[0], r2.at[1]
        for g, (lo, n) in enumerate(spans):
            axis, reg = ORDERS[g][phase], regs[g]
            right, left = h.nbr(axis, 1), h.nbr(axis, 3)
            p0, p1 = halves(lo, n)
            R = lambda part, d: cut(reg(pl.ds(*part[:2]), h.at(axis, d)), part)
            T = lambda ref, part: cut(take(ref, pl.ds(*part[:2])), part)
            s.first += [rcopy(R(p0, 2), T(r1, p0), ss, rs.at[0], right), rcopy(R(p1, 2), T(r1, p1), ss, rs.at[0], left)]
            s.second += [rcopy(R(p1, 1), T(l, p1), ss, rs.at[1], right), rcopy(R(p0, 3), T(r, p0), ss, rs.at[1], left)]
            s.third += [rcopy(R(p0, 1), T(l, p0), ss, rs.at[1], right), rcopy(R(p1, 3), T(r, p1), ss, rs.at[1], left)]
            s.parts += [(p0, reg, h.at(axis, 1)), (p1, reg, h.at(axis, 3))]
            s.items.append((lo, n, reg, h.c[axis]))
    def start(s):
        for c in s.first + s.second: c.start()
    def add(s, part, reg, v):
        def one(k):
            ref, got = reg(k, v), s.take(s.r1, k)
            if part[2] is not None: ref, got = (x.at[pl.ds(112 * part[2], 112)] for x in (ref, got))
            ref[...] = (ref[...].astype(F32) + got[...].astype(F32)).astype(BF)
        if part[1] == 1: one(part[0])
        else: pl.loop(0, part[1])(lambda i: one(part[0] + i))
    def relay(s):
        take_bytes(s.size(1, s.n), s.rs.at[0], s.h)
        for p, c in zip(s.parts, s.third):
            s.add(*p); c.start()
    def total(s, k, reg, v):
        return reg(k, v)[...].astype(F32) + s.take(s.r2.at[0], k)[...].astype(F32) + s.take(s.r2.at[1], k)[...].astype(F32)
    def arrive(s): take_bytes(s.size(2, s.n), s.rs.at[1], s.h)

def take0(ref, k): return ref.at[k]
def take1(ref, k): return ref.at[:, k]

class Layer:
    def __init__(s, **kw): s.__dict__.update(kw)

    def reg3(s, g): return lambda sl, v: s.w.at[sl, v]
    def reg2(s, g): return lambda sl, v: s.pb.at[v, :, sl]
    def reg1(s, g): return lambda sl, v: s.pb.at[s.h.c[ORDERS[g][1]], v, sl]
    def span(s, g, k):
        if isinstance(k, int):
            return ATT[g] if k < 0 else (FFN[g], 1) if k == 0 else (FFN[g] + 2 * k - 1, 2)
        return FFN[g] + 2 * k - 1, 2
    def size3(s, m, n): return s.r1a.at[pl.ds(0, n)] if m == 1 else s.r2a.at[:, pl.ds(0, n)]
    def size2(s, m, n): return s.r1b.at[:, pl.ds(0, n)] if m == 1 else s.r2b.at[:, :, pl.ds(0, n)]
    def size1(s, m, n): return s.r1c.at[pl.ds(0, n)] if m == 1 else s.r2c.at[:, pl.ds(0, n)]
    def regs(s, p): return [(s.reg1, s.reg2, s.reg3)[p](g) for g in range(3)]
    def wave(s, waves, g, i): return ATT[g] if i == 0 else (FFN[g] + waves[i - 1][0], waves[i - 1][1])
    def spans(s, waves, i): return [s.wave(waves, g, i) for g in range(3)]
    def ring1(s, i): return Rings(s.h, s.regs(0), 0, s.spans(GATHER_WAVES, i), s.gss.at[0], s.grs.at[i], s.size1)
    def ring2(s, i): return Rings(s.h, s.regs(1), 1, s.spans(GATHER_WAVES, i), s.gss.at[1], s.grs.at[3 + i], s.size2)
    def ring3(s, k): return Rings(s.h, s.regs(2), 2, [s.span(g, k) for g in range(3)], s.gss.at[2], s.grs.at[7 + k], s.size3)
    def compact(s, k):
        for g in range(3):
            lo, n = s.span(g, k)
            c = s.h.c[ORDERS[g][2]]
            for i in range(0, n, 2):
                m = min(2, n - i)
                x = lanes([s.pb[:, :, lo + i + j].reshape(256, 128) for j in range(m)])
                y = nn(s.cmat[...], x).astype(BF)
                for j in range(m): s.w[lo + i + j, c] = y[:, 128 * j:128 * j + 128]
    def send3(s, k):
        s.compact(k)
        s.ring3(k).start()
    def relay3(s, k): s.ring3(k).relay()
    def finish3(s, k): s.ring3(k).finish()

    def fold3(s, k):
        return Folds(s.h, s.regs(2), 2, [s.span(g, k) for g in range(3)], s.r1a, s.r2a, s.fss.at[2], s.frs.at[k + 1], take0, s.size3)
    def fold2(s, i): return Folds(s.h, s.regs(1), 1, s.spans(SUM_WAVES, i), s.r1b, s.r2b, s.fss.at[1], s.frs.at[11 + i], take1, s.size2)
    def fold1(s, i): return Folds(s.h, s.regs(0), 0, s.spans(SUM_WAVES, i), s.r1c, s.r2c, s.fss.at[0], s.frs.at[14 + i], take0, s.size1)
    def fold_start(s, k): s.fold3(k).start()
    def fold_relay(s, k): s.fold3(k).relay()
    def fold_expand(s, k):
        f = s.fold3(k)
        f.arrive()
        for lo, n, reg, v in f.items:
            for i in range(0, n, 2):
                m = min(2, n - i)
                x = lanes([f.total(lo + i + j, reg, v).astype(BF) for j in range(m)])
                y = nn(s.emat[...], x).astype(BF)
                for j in range(m): s.pb[:, :, lo + i + j] = y[:, 128 * j:128 * j + 128].reshape(4, 4, 16, 128)
    def settle2(s, f):
        f.arrive()
        for lo, n, reg, v in f.items:
            @pl.loop(0, n)
            def _(i): s.pb[v, :, lo + i] = f.total(lo + i, reg, v).astype(BF)
    def settle1(s, f):
        f.arrive()
        for lo, n, reg, v in f.items:
            @pl.loop(0, n)
            def _(i): s.grads[lo + i] = f.total(lo + i, reg, v)
    def sent(s, sems):
        for ref, i in ((s.pb.at[0, pl.ds(0, 3)], 0), (s.pb.at[pl.ds(0, 3)], 1), (s.w.at[:, pl.ds(0, 3)], 2)):
            take_bytes(ref, sems.at[i], s.h)

    def small(s, t, p):
        a = AX[p]
        own = s.slots.at[t, p, s.h.c[a]]
        return [rcopy(own, own, s.sss.at[0], s.srs.at[t, p], s.h.nbr(a, d)) for d in (1, 2, 3)]
    def small_start(s, t, p, v):
        s.slots[t, p, s.h.c[AX[p]]] = v
        for c in s.small(t, p): c.start()
    def small_end(s, t, p):
        q = s.slots.at[t, p]
        take_bytes(q.at[pl.ds(0, 3)], s.srs.at[t, p], s.h)
        return (q[0] + q[1]) + (q[2] + q[3])

    def slab(s, k): return s.w[k].reshape(W, 128)
    def codes(s, lo, n): return lanes([s.slab(lo + i) for i in range(n)])
    def pair(s, k, lo, n):
        d = pl.ds(lo, n)
        return rcopy(s.xs.at[d], s.xr.at[k % 2, d], s.xss.at[k, lo // 128], s.xrs.at[k, lo // 128], (s.h.dp, 1 - s.h.mp))
    def offer(s, k, part, lo=0):
        s.xs[pl.ds(lo, part.shape[0])] = part.astype(BF)
        s.pair(k, lo, part.shape[0]).start()
    def accept(s, k, n, lo=0):
        s.pair(k, lo, n).wait()
        return s.xs[pl.ds(lo, n)].astype(F32) + s.xr[k % 2, pl.ds(lo, n)].astype(F32)
    def exchange(s, k, part):
        s.offer(k, part)
        return s.accept(k, part.shape[0])

    def matrices(s):
        i, j = iota((224, 256), 0), iota((224, 256), 1)
        s.cmat[...] = jnp.where(j == i + 2 * lax.shift_right_logical(i * 4682, 16), 1.0, 0.0).astype(BF)
        i, j = iota((256, 224), 1), iota((256, 224), 0)
        s.emat[...] = jnp.where(j == i + 2 * lax.shift_right_logical(i * 4682, 16), 1.0, 0.0).astype(BF)

    def row(s, r): return r[...].reshape(1, r.shape[0])

    def prologue(s):
        i = iota((W, 1), 0)
        blk = lax.shift_right_logical(i * 4682, 16)
        r = i - 14 * blk
        c = {"x": lax.shift_right_logical(blk, 4), "y": jnp.bitwise_and(lax.shift_right_logical(blk, 2), 3), "z": jnp.bitwise_and(blk, 3)}
        j = iota((W, W), 1)
        for g in range(2):
            a1, a2, a3 = (c[a] for a in ORDERS[g])
            s.q[g] = jnp.where(j == ((a3 * 4 + a2) * 4 + a1) * 14 + r, 1.0, 0.0).astype(BF)
        l0, l1 = s.lengths[0, 0], s.lengths[0, 1]
        def seg_of(i): return jnp.where(i >= l0, 1, 0) + jnp.where(i >= l0 + l1, 1, 0)
        ti, tj = iota((128, 128), 0), iota((128, 128), 1)
        si, sj = seg_of(ti), seg_of(tj)
        s.allow[...] = jnp.where((si == sj) & (tj <= ti), 1.0, 0.0)
        pos = ti - jnp.where(si == 0, 0, jnp.where(si == 1, l0, l0 + l1))
        lane = jnp.bitwise_and(tj, 31).astype(F32)
        ang = pos.astype(F32) * jnp.exp(lane * (-math.log(10000.0) / 32))
        co, sn = jnp.cos(ang), jnp.sin(ang)
        sn = jnp.where(jnp.bitwise_and(tj, 63) < 32, -sn, sn)
        s.cos[...] = co
        s.sin[...] = sn
        x = s.hidden[...].astype(F32)
        nrm = (x * rinv(x) * s.gains[0:1]).astype(BF)
        s.nrm[2] = nrm
        for g in range(2): s.nrm[g] = nn(nrm, s.q[g]).astype(BF)
        s.qkvs[...] = jnp.zeros_like(s.qkvs)
        s.qkvs[:, 0:576] = lanes([s.row(r) for r in (s.q_scale, s.k_scale, s.v_scale)])
        for to, r in ((s.osc, s.o_scale), (s.gsc, s.g_scale), (s.usc, s.u_scale), (s.dsc, s.d_scale)): to[...] = s.row(r)

    def swap(s, v):
        lane = jnp.bitwise_and(iota((128, 512), 1), 63)
        return jnp.where(lane < 32, pltpu.roll(v, 512 - 32, 1), pltpu.roll(v, 32, 1))

    def probs(s, qs, k):
        th = jnp.tanh(nt(qs, k) * (0.125 / CAP))
        e = jnp.exp(CAP * th) * rows([s.allow[...]] * 7)
        return th, e / jnp.sum(e, axis=-1, keepdims=True)

    def heads(s, qk): return rows([qk[:, 64 * i:64 * i + 64] for i in range(7)]), qk[:, 448:512]

    def attention(s, b):
        rs = rsum(s.nrm[2])
        lin = lanes([nn(s.nrm[0], units(s.codes(0, 2), b)), nn(s.nrm[1], units(s.codes(2, 2), b)), nn(s.nrm[2], units(s.codes(4, 1), b))])
        lin = (lin * MUL[b] + OFF[b] * rs) * s.qkvs[...]
        s.lin[b] = lin.astype(s.lin.dtype)
        qk = lin[:, :512]
        qk = (qk * lanes([s.cos[...]] * 4) + s.swap(qk) * lanes([s.sin[...]] * 4)).astype(BF)
        qs, k = s.heads(qk)
        v = lin[:, 512:576].astype(BF)
        s.qk[b], s.v[b] = qk, v
        _, pr = s.probs(qs, k)
        mx = nn(pr.astype(BF), v).astype(BF)
        mixed = lanes([jnp.zeros((128, 64), BF)] + [mx[128 * i:128 * i + 128] for i in range(7)])
        d = pl.ds(128 * b, 128)
        s.mixed[d] = mixed
        s.acc[0, d] = nt(mixed, units(s.codes(4, 4), b)) * MUL[b] + OFF[b] * rsum(mixed)

    def lifted(s, b):
        br = s.bu[pl.ds(128 * b, 128)] * s.osc[...]
        r = rinv(br)
        return s.hidden[...].astype(F32) + br * r * s.gains[1:2], br, r

    def middle(s):
        s.bu[...] = s.exchange(0, s.acc[0])
        for b in range(3):
            d = pl.ds(128 * b, 128)
            lif = s.lifted(b)[0]
            n2 = (lif * rinv(lif) * s.gains[2:3]).astype(BF)
            s.rsn[d] = jnp.broadcast_to(rsum(n2), (128, 128))
            for g in range(2): s.n2[g, d] = nn(n2, s.q[g]).astype(BF)
        for g in range(2): s.n2t[g] = s.n2[g].T
        s.acc[0] = jnp.zeros((384, W), F32)
        s.asum[...] = jnp.zeros_like(s.asum)

    def srow(s, ref, k, n): return ref[:, pl.ds(128 * k if isinstance(k, int) else pl.multiple_of(k * 128, 128), n * 128)]

    def ffn_fwd(s, k, n, last=False):
        wg, wu, wd = (s.codes(f + k, n) for f in FFN)
        sg, su = s.srow(s.gsc, k, n), s.srow(s.usc, k, n)
        for b in range(3):
            d = pl.ds(128 * b, 128)
            rs = s.rsn[d][:, 0:1] * OFF[b]
            g = (nn(s.n2[0, d], units(wg, b)) * MUL[b] + rs) * sg
            u = (nn(s.n2[1, d], units(wu, b)) * MUL[b] + rs) * su
            act = (0.5 * g * (1.0 + jnp.tanh(C0 * (g + C1 * g * g * g))) * u).astype(BF)
            for i in range(n):
                c = slice(128 * i, 128 * i + 128)
                s.g[k + i, d], s.u[k + i, d] = g[:, c].astype(BF), u[:, c].astype(BF)
            s.acc[0, d] += nt(act, units(wd, b))
            s.asum[0, d] += jnp.broadcast_to(rsum(act) * OFF[b], (128, 128))
            if last: s.offer(1, s.acc[0, d] * MUL[b] + s.asum[0, d][:, 0:1], 128 * b)

    def scaled(s, g):
        return rows([s.acc[g, pl.ds(128 * b, 128)] * MUL[b] for b in range(3)]) + s.asum[g][:, 0:1]

    def turn(s):
        dgain, dsd = 0.0, 0.0
        for b in range(3):
            d = pl.ds(128 * b, 128)
            f = s.accept(1, 128, 128 * b)
            feed = f * s.dsc[...]
            r = rinv(feed)
            s.result[b] = (s.lifted(b)[0] + feed * r * s.gains[3:4]).astype(BF)
            df, dg = rms_back(feed, r, s.gains[3:4], s.cot[b].astype(F32))
            dgain += dg
            dfl = df.astype(BF)
            dsd += csum(dfl.astype(F32) * f)
            s.n2[0, d] = dfl
            dfs = (df * s.dsc[...]).astype(BF)
            s.n2[1, d] = dfs
            s.rsn[d] = jnp.broadcast_to(rsum(dfs) * OFF[b], (128, 128))
        s.sm[11:12] = dgain
        s.sm[7:8] = dsd
        s.dft[...] = s.n2[0].T
        s.acc[...] = jnp.zeros_like(s.acc)
        s.asum[...] = jnp.zeros_like(s.asum)

    def ffn_dx(s, k, n):
        wg, wu, wd = (s.codes(f + k, n) for f in FFN)
        sg, su = s.srow(s.gsc, k, n), s.srow(s.usc, k, n)
        al = []
        gsum, usum = 0.0, 0.0
        get = lambda ref, d: lanes([ref[k + i, d] for i in range(n)])
        for b in range(3):
            d = pl.ds(128 * b, 128)
            da = nn(s.n2[1, d], units(wd, b)) * MUL[b] + s.rsn[d][:, 0:1]
            g, u = get(s.g, d).astype(F32), get(s.u, d).astype(F32)
            t = jnp.tanh(C0 * (g + C1 * g * g * g))
            hp = 0.5 * (1.0 + t)
            gelu = g * hp
            du = da * gelu
            dg = da * u * (hp + 0.5 * g * (1.0 - t * t) * C0 * (1.0 + 3 * C1 * g * g))
            dgl, dul = dg.astype(BF), du.astype(BF)
            al.append((gelu * u).astype(BF))
            for i in range(n):
                c = slice(128 * i, 128 * i + 128)
                s.g[k + i, d], s.u[k + i, d] = dgl[:, c], dul[:, c]
            gsum += csum(dgl.astype(F32) * g); usum += csum(dul.astype(F32) * u)
            dgs, dus = (dg * sg).astype(BF), (du * su).astype(BF)
            s.acc[0, d] += nt(dgs, units(wg, b))
            s.acc[1, d] += nt(dus, units(wu, b))
            s.asum[0, d] += jnp.broadcast_to(rsum(dgs) * OFF[b], (128, 128))
            s.asum[1, d] += jnp.broadcast_to(rsum(dus) * OFF[b], (128, 128))
        at = lambda ref: ref.at[:, pl.ds(128 * k if isinstance(k, int) else pl.multiple_of(k * 128, 128), n * 128)]
        at(s.gsg)[...] = gsum / sg
        at(s.usg)[...] = usum / su
        s.put(2, k, n, nn(s.dft[...], rows(al)))

    def put(s, g, k, n, dw):
        dw = dw.astype(BF)
        for i in range(n): s.w[FFN[g] + k + i] = dw[:, 128 * i:128 * i + 128].reshape(4, 224, 128)
    def ffn_dw(s, k, n):
        for g, ref in enumerate((s.g, s.u)): s.put(g, k, n, nn(s.n2t[g], lanes([ref[k + i] for i in range(n)])))

    def pack(s):
        for i in range(3):
            m = min(W, 2432 - W * i)
            s.sm[i:i + 1, 0:m] = s.gsg[:, W * i:W * i + m]
            s.sm[3 + i:4 + i, 0:m] = s.usg[:, W * i:W * i + m]

    def lower(s):
        s.offer(2, sum(nt(s.scaled(g).astype(BF), s.q[g]) for g in range(2)))
        s.fill()
        dn = s.accept(2, 384)
        dg1, dg2, dso, din = 0.0, 0.0, 0.0, 0.0
        for b in range(3):
            d = pl.ds(128 * b, 128)
            lif, br, r = s.lifted(b)
            dl, dg = rms_back(lif, rinv(lif), s.gains[2:3], dn[128 * b:128 * b + 128])
            dg2 += dg
            dl = dl + s.cot[b].astype(F32)
            din = din + dl
            db, dg = rms_back(br, r, s.gains[1:2], dl)
            dg1 += dg
            dbl = db.astype(BF)
            dso += csum(dbl.astype(F32) * s.bu[d])
            s.n2[0, d] = dbl
            s.n2[1, d] = (db * s.osc[...]).astype(BF)
        s.din[...] = din
        s.sm[9:10], s.sm[10:11], s.sm[6:7] = dg1, dg2, dso

    def attention_back(s, b):
        d = pl.ds(128 * b, 128)
        dbs = s.n2[1, d]
        dm = (nn(dbs, units(s.codes(4, 4), b)) * MUL[b] + OFF[b] * rsum(dbs)).astype(BF)
        dms = rows([dm[:, 64 * i + 64:64 * i + 128] for i in range(7)])
        v = s.v[b]
        qs, k = s.heads(s.qk[b])
        th, pr = s.probs(qs, k)
        dp = nt(dms, v)
        gv = tn(pr.astype(BF), dms)
        dc = pr * (dp - jnp.sum(dp * pr, axis=-1, keepdims=True))
        dr = (dc * (1.0 - th * th)).astype(BF)
        gq = nn(dr, k) * 0.125
        gk = tn(dr, qs) * 0.125
        gqk = lanes([gq[128 * i:128 * i + 128] for i in range(7)] + [gk])
        gqk = gqk * lanes([s.cos[...]] * 4) - s.swap(gqk) * lanes([s.sin[...]] * 4)
        g = lanes([gqk, gv, jnp.zeros((128, 64), F32)])
        gl = g.astype(BF).astype(F32)
        gs = (g * s.qkvs[...]).astype(BF)
        sg = csum(gl * s.lin[b].astype(F32))
        for i, (c, lo, n) in enumerate(((slice(0, 256), 0, 2), (slice(256, 512), 2, 2), (slice(512, 640), 4, 1))):
            part = nt(gs[:, c], units(s.codes(lo, n), b)) * MUL[b] + rsum(gs[:, c]) * OFF[b]
            e = pl.ds(128 * i, 128)
            if b: s.acc[0, e] += part
            else: s.acc[0, e] = part
        if b:
            s.dqk[...] += gl; s.sqk[...] += sg
        else:
            s.dqk[...] = gl; s.sqk[...] = sg

    def attention_grads(s):
        sc = s.qkvs[...]
        s.sm[12:13, 0:640] = jnp.where(sc > 0, s.sqk[...] / sc, 0.0)
        dqk = s.dqk[...].astype(BF)
        dw = [nn(s.nrm[0].T, dqk[:, 0:256]), nn(s.nrm[1].T, dqk[:, 256:512])]
        lhs = lanes([s.nrm[2].T, s.n2[0].T])
        rhs = rows([lanes([dqk[:, 512:576], jnp.zeros((128, 448), BF)]), s.mixed[...]])
        dw.append(nn(lhs, rhs))
        for (lo, n), x in zip(ATT, dw):
            x = x.astype(BF)
            for i in range(n): s.w[lo + i] = x[:, 128 * i:128 * i + 128].reshape(4, 224, 128)

    def last_offer(s):
        s.offer(3, sum(nt(s.acc[0, pl.ds(128 * g, 128)].astype(BF), s.q[g]) for g in range(2)) + s.acc[0, pl.ds(256, 128)])
    def last(s):
        dn = s.accept(3, 128)
        x = s.hidden[...].astype(F32)
        dx, dg = rms_back(x, rinv(x), s.gains[0:1], dn)
        s.sm[8:9] = dg
        s.in_grad[...] = (s.din[...] + dx).astype(BF)

LOADS = ("hidden", "cot", "lengths", "gains", "q_scale", "k_scale", "v_scale", "o_scale", "g_scale", "u_scale", "d_scale")
STORES = ("grads", "smo", "result", "in_grad")
INS = ("block",) + tuple(n + "_in" for n in LOADS)
OUTS = tuple(n + "_out" for n in STORES)
def scratch():
    V, D = pltpu.VMEM, pltpu.SemaphoreType.DMA
    return dict(
        hidden=V((128, W), BF), cot=V((3, 128, W), BF), lengths=pltpu.SMEM((1, 3), jnp.int32), gains=V((4, W), F32),
        q_scale=V((448,), F32), k_scale=V((64,), F32), v_scale=V((64,), F32), o_scale=V((W,), F32), g_scale=V((2432,), F32),
        u_scale=V((2432,), F32), d_scale=V((W,), F32), grads=V((65, 16, 128), F32), smo=V((16, W), F32), result=V((3, 128, W), BF),
        in_grad=V((128, W), BF), isem=D((len(LOADS),)), osem=D((len(STORES) + 2,)),
        w=V((65, 4, 224, 128), BF), pb=V((4, 4, 65, 16, 128), BF),
        r1a=V((65, 224, 128), BF), r2a=V((2, 65, 224, 128), BF), r1b=V((4, 65, 16, 128), BF), r2b=V((2, 4, 65, 16, 128), BF),
        r1c=V((65, 16, 128), BF), r2c=V((2, 65, 16, 128), BF), slots=V((2, 3, 4, 8, W), F32), sm=V((16, W), F32),
        cmat=V((224, 256), BF), emat=V((256, 224), BF), q=V((2, W, W), BF), allow=V((128, 128), F32), cos=V((128, 128), F32),
        sin=V((128, 128), F32), nrm=V((3, 128, W), BF), qkvs=V((1, 640), F32), lin=V((3, 128, 640), BF), qk=V((3, 128, 512), BF),
        v=V((3, 128, 64), BF), mixed=V((384, 512), BF), acc=V((2, 384, W), F32), bu=V((384, W), F32),
        n2=V((2, 384, W), BF), n2t=V((2, W, 384), BF), rsn=V((384, 128), F32), asum=V((2, 384, 128), F32),
        g=V((19, 384, 128), BF), u=V((19, 384, 128), BF), dft=V((W, 384), BF),
        gsg=V((1, 2432), F32), usg=V((1, 2432), F32), din=V((128, W), F32), dqk=V((128, 640), F32),
        sqk=V((1, 640), F32), osc=V((1, W), F32), dsc=V((1, W), F32), gsc=V((1, 2432), F32), usc=V((1, 2432), F32), xs=V((384, W), BF), xr=V((2, 384, W), BF), xss=D((4, 3)), xrs=D((4, 3)),
        gss=D((3,)), grs=D((17, 2)), fss=D((3,)), frs=D((17, 2)), sss=D((1,)), srs=D((2, 3)), lsem=D((6,)))

def body(names, *refs):
    h = Here()
    s = Layer(h=h, **dict(zip(names, refs)))
    loads = [pltpu.make_async_copy(getattr(s, n + "_in"), getattr(s, n), s.isem.at[i]) for i, n in enumerate(LOADS)]
    stores = []
    def store(i, n, part=None):
        a, b = getattr(s, n), getattr(s, n + "_out")
        if part is not None: a, b = a.at[pl.ds(*part)], b.at[pl.ds(*part)]
        stores.append(pltpu.make_async_copy(a, b, s.osem.at[i]))
        stores[-1].start()
    local = []
    for g in range(3):
        a1, a2, _ = ORDERS[g]
        for i, (lo, n) in enumerate((ATT[g], (FFN[g], 19))):
            local.append(pltpu.make_async_copy(s.block.at[pl.ds(lo, n)], s.pb.at[h.c[a2], h.c[a1], pl.ds(lo, n)], s.lsem.at[2 * g + i]))
    for c in local + loads: c.start()
    bar = pltpu.get_barrier_semaphore()
    for a in AX:
        for d in (1, 2, 3):
            pl.semaphore_signal(bar, inc=1, device_id=h.nbr(a, d), device_id_type=MESH)
    pl.semaphore_signal(bar, inc=1, device_id=(h.dp, 1 - h.mp), device_id_type=MESH)
    pl.semaphore_wait(bar, 10)
    for c in local: c.wait()
    one, two = [s.ring1(i) for i in range(3)], [s.ring2(i) for i in range(3)]
    def do(what, r): getattr(r, what)()
    for i in range(3): do("start", one[i])
    s.matrices()
    do("relay", one[0])
    do("relay", one[1])
    do("finish", one[0])
    do("start", two[0])
    do("relay", one[2])
    do("finish", one[1])
    do("start", two[1])
    s.sm[...] = jnp.zeros_like(s.sm)
    do("relay", two[0])
    do("finish", one[2])
    do("start", two[2])
    for c in loads: c.wait()
    s.prologue()
    do("finish", two[0])
    s.send3(-1)
    do("relay", two[1])
    do("finish", two[1])
    s.send3(0); s.send3(1)
    s.relay3(-1)
    do("relay", two[2])
    s.send3(2)
    s.finish3(-1)
    s.attention(0)
    s.relay3(0); s.send3(3)
    do("finish", two[2])
    s.attention(1)
    s.relay3(1); s.send3(4)
    s.attention(2)
    s.relay3(2); s.send3(5)
    s.middle()
    s.relay3(3); s.send3(6)
    s.finish3(0)
    s.ffn_fwd(0, 1)
    @pl.loop(1, NCH - 1)
    def _(k):
        @pl.when(k < NCH - 3)
        def _(): s.relay3(k + 3)
        @pl.when(k < NCH - 6)
        def _(): s.send3(k + 6)
        s.finish3(k)
        s.ffn_fwd(2 * k - 1, 2)
    s.finish3(NCH - 1)
    s.ffn_fwd(17, 2, last=True)
    s.turn()
    store(2, "result")
    s.sent(s.gss)
    def emit(k):
        s.ffn_dw(2 * k - 1, 2)
        s.fold_start(k)
    s.ffn_dx(0, 1)
    s.ffn_dw(0, 1)
    s.fold_start(0)
    @pl.loop(1, 7)
    def _(k):
        s.ffn_dx(2 * k - 1, 2)
        emit(k)
        @pl.when(k == 2)
        def _(): s.fold_relay(0)
        @pl.when(k > 2)
        def _(): s.fold_relay(k - 2)
    @pl.loop(7, NCH)
    def _(k):
        s.ffn_dx(2 * k - 1, 2)
        @pl.when(k < 9)
        def _(): s.fold_relay(k - 2)
    s.pack()
    s.fill = lambda: emit(7)
    s.lower()
    s.small_start(0, 0, s.sm[0:8])
    f2, f1 = [s.fold2(i) for i in range(3)], [s.fold1(i) for i in range(3)]
    s.attention_back(0)
    emit(8)
    s.attention_back(1)
    s.fold_relay(7)
    emit(9)
    s.attention_back(2)
    s.attention_grads()
    s.fold_start(-1)
    s.last_offer()
    s.fold_relay(8)
    s.fold_expand(0)
    @pl.loop(1, 5)
    def _(k): s.fold_expand(k)
    do("start", f2[1])
    s.fold_relay(9)
    s.last()
    store(3, "in_grad")
    s.small_start(1, 0, s.sm[8:16])
    s.small_start(0, 1, s.small_end(0, 0))
    s.fold_expand(5)
    s.fold_expand(6)
    s.fold_relay(-1)
    do("relay", f2[1])
    @pl.loop(7, NCH)
    def _(k): s.fold_expand(k)
    do("start", f2[2])
    s.fold_expand(-1)
    do("start", f2[0])
    s.settle2(f2[1])
    do("start", f1[1])
    s.small_start(0, 2, s.small_end(0, 1))
    do("relay", f2[2])
    do("relay", f2[0])
    s.small_start(1, 1, s.small_end(1, 0))
    s.settle2(f2[0])
    do("start", f1[0])
    do("relay", f1[1])
    s.settle2(f2[2])
    do("start", f1[2])
    do("relay", f1[0])
    s.small_start(1, 2, s.small_end(1, 1))
    s.settle1(f1[1])
    do("relay", f1[2])
    s.settle1(f1[0])
    s.settle1(f1[2])
    s.smo[0:8] = s.small_end(0, 2)
    s.smo[8:16] = s.small_end(1, 2)
    store(1, "smo")
    store(0, "grads")
    s.sent(s.fss)
    for c in stores: c.wait()
    take_bytes(s.slots.at[:, :, pl.ds(0, 3)], s.sss.at[0], s.h)

def layer(*ins):
    A = pl.BlockSpec(memory_space=pl.ANY)
    sc = scratch()
    return pl.pallas_call(
        functools.partial(body, INS + OUTS + tuple(sc)),
        out_shape=(jax.ShapeDtypeStruct((65, 16, 128), F32), jax.ShapeDtypeStruct((16, W), F32), jax.ShapeDtypeStruct((3, 128, W), BF),
                   jax.ShapeDtypeStruct((128, W), BF)),
        in_specs=[A] * len(INS), out_specs=(A,) * 4, scratch_shapes=list(sc.values()),
        compiler_params=pltpu.CompilerParams(collective_id=0, has_side_effects=True, vmem_limit_bytes=63 << 20),
    )(*ins)

SHAPES = [(14, 448), (14, 64), (14, 64), (14, 448), (14, 2432), (14, 2432), (14, 2432), (448,), (64,), (64,), (896,), (2432,), (2432,), (896,), (4, 896)]

def unpack_body(*refs):
    ins, outs, own, (g_ref, sm_ref, isem, osem) = refs[:4], refs[4:21], refs[21:38], refs[38:]
    cs = [pltpu.make_async_copy(x, y, isem.at[i]) for i, (x, y) in enumerate(zip(ins, (g_ref, sm_ref) + own[:2]))]
    out = [pltpu.make_async_copy(x, y, osem.at[i]) for i, (x, y) in enumerate(zip(own, outs))]
    for c in cs: c.start()
    (q, k, v, o, gate, up, down), vecs, gains = own[2:9], own[9:16], own[16]
    for i in range(2):
        cs[2 + i].wait(); out[i].start()
    for i in range(2): cs[i].wait()
    cat = lambda lo, n: lanes([g_ref[i] for i in range(lo, lo + n)])[:14]
    for i, (ref, f) in enumerate(zip((gate, up, down), FFN)):
        ref[...] = cat(f, 19)
        out[6 + i].start()
    att = cat(0, 8)
    q[...], k[...], v[...], o[...] = att[:, :448], att[:, 448:512], att[:, 512:576], att[:, 576:]
    for i in range(2, 6): out[i].start()
    long = lambda r: lanes([sm_ref[r:r + 1], sm_ref[r + 1:r + 2], sm_ref[r + 2:r + 3, 0:640]])
    parts = (sm_ref[12:13, 0:448], sm_ref[12:13, 448:512], sm_ref[12:13, 512:576], sm_ref[6:7], long(0), long(3), sm_ref[7:8])
    for ref, row in zip(vecs, parts): ref[...] = row.reshape(ref.shape[0])
    gains[...] = sm_ref[8:12]
    for c in out[9:]: c.start()
    for c in out: c.wait()

def unpack(*a):
    A, V, D = pl.BlockSpec(memory_space=pl.ANY), pltpu.VMEM, pltpu.SemaphoreType.DMA
    outs = [jax.ShapeDtypeStruct(x.shape, BF) for x in a[2:]] + [jax.ShapeDtypeStruct(x, F32) for x in SHAPES]
    return pl.pallas_call(unpack_body, out_shape=outs, in_specs=[A] * 4, out_specs=[A] * len(outs),
                          scratch_shapes=[V(x.shape, x.dtype) for x in outs] + [V((65, 16, 128), F32), V((16, W), F32), D((4,)), D((17,))],
                          compiler_params=pltpu.CompilerParams(vmem_limit_bytes=63 << 20))(*a)

def local(hidden_in, cotangent, lengths, gains, query_codes, key_codes, value_codes, output_codes, gate_codes, upward_codes, down_codes,
          query_scale, key_scale, value_scale, output_scale, gate_scale, upward_scale, down_scale):
    block = jnp.concatenate([query_codes, key_codes, value_codes, output_codes.T, gate_codes, upward_codes, down_codes.T], axis=1)
    block = jnp.pad(block, ((0, 2), (0, 0))).reshape(16, 65, 128).transpose(1, 0, 2)
    out = layer(block, hidden_in, cotangent, lengths, gains, query_scale, key_scale, value_scale, output_scale, gate_scale, upward_scale, down_scale)
    out = unpack(*out)
    return (*out[:5], out[5].T, *out[6:8], out[8].T, *out[9:])

def solution(mesh):
    d, c, r = P("dp", None), P("dp", "mp"), P("mp", "dp")
    return jax.shard_map(local, mesh=mesh,
        in_specs=(d, P(None, "dp", None), d, P(), c, c, c, r, c, c, r, P("mp"), P("mp"), P("mp"), P(), P("mp"), P("mp"), P()),
        out_specs=(P(None, "dp", None), d, c, c, c, r, c, c, r, P("mp"), P("mp"), P("mp"), P(), P("mp"), P("mp"), P(), P()),
        check_vma=False)
```

```python
import functools
import math

import jax
import jax.numpy as jnp
from jax import lax
from jax.experimental import pallas as pl
from jax.experimental.pallas import tpu as pltpu
from jax.sharding import PartitionSpec as P
MESH = pl.DeviceIdType.MESH
F32, BF = jnp.float32, jnp.bfloat16
STRIDE = {"x": 16, "y": 4, "z": 1}
AX = "xyz"
ORDERS = ("xzy", "yxz", "zyx")
ATT = ((0, 2), (2, 2), (4, 4))
FFN = (8, 27, 46)
GATHER_WAVES = ((0, 7), (7, 12))
SUM_WAVES = ((0, 7), (7, 6), (13, 6))
NCH = 10
MUL = (1.0, 16.0, 64.0)
OFF = (-127.5, -120.0, -96.0)
EPS, CAP = 1e-6, 50.0
C0, C1 = math.sqrt(2 / math.pi), 0.044715
W = 896

def nn(a, b): return lax.dot_general(a, b, (((1,), (0,)), ((), ())), preferred_element_type=F32)
def nt(a, b): return lax.dot_general(a, b, (((1,), (1,)), ((), ())), preferred_element_type=F32)
def tn(a, b): return lax.dot_general(a, b, (((0,), (0,)), ((), ())), preferred_element_type=F32)
def iota(s, d): return lax.broadcasted_iota(jnp.int32, s, d)
def rsum(a): return jnp.sum(a.astype(F32), axis=-1, keepdims=True)
def csum(a): return jnp.sum(a, axis=0, keepdims=True)
def units(c, b): return c if b == 0 else jnp.floor(c * BF(1 / MUL[b]))
def rinv(v): return lax.rsqrt(jnp.sum(v * v, axis=-1, keepdims=True) * (1 / W) + EPS)
def rms_back(v, r, gain, dy):
    gd = gain * dy
    m = jnp.sum(v * gd, axis=-1, keepdims=True) * (1 / W)
    return r * gd - v * (r * r * r * m), csum(dy * v * r)
def lanes(a): return jnp.concatenate(a, axis=1)
def rows(a): return jnp.concatenate(a, axis=0)

class Here:
    def __init__(s):
        s.dp = lax.axis_index("dp"); s.mp = lax.axis_index("mp")
        s.c = {a: lax.rem(s.dp // STRIDE[a], 4) for a in AX}
    def nbr(s, a, d):
        c = s.c[a]
        return (s.dp + (lax.rem(c + d, 4) - c) * STRIDE[a], s.mp)
    def at(s, a, d):
        return lax.rem(s.c[a] + d, 4)

def rcopy(src, dst, ss, rs, dev):
    return pltpu.make_async_remote_copy(src_ref=src, dst_ref=dst, send_sem=ss, recv_sem=rs, device_id=dev, device_id_type=MESH)

def halves(lo, n):
    if n == 1: return (lo, 1, 0), (lo, 1, 1)
    return (lo, n // 2, None), (lo + n // 2, n - n // 2, None)
def cut(ref, part): return ref if part[2] is None else ref.at[:, pl.ds(112 * part[2], 112)]

def take_bytes(ref, sem, h):
    rcopy(ref, ref, sem, sem, (h.dp, 1 - h.mp)).wait_recv()

class Rings:
    def __init__(s, h, regs, phase, spans, ss, rs, size):
        s.h, s.ss, s.rs, s.size, s.n = h, ss, rs, size, sum(n for _, n in spans)
        s.a, s.b = [], []
        for g, (lo, n) in enumerate(spans):
            axis, reg = ORDERS[g][phase], regs[g]
            right, left = h.nbr(axis, 1), h.nbr(axis, 3)
            p0, p1 = halves(lo, n)
            r = reg(pl.ds(lo, n), h.c[axis])
            r0 = cut(reg(pl.ds(*p0[:2]), h.at(axis, 3)), p0)
            r1 = cut(reg(pl.ds(*p1[:2]), h.at(axis, 1)), p1)
            s.a += [rcopy(r, r, ss, rs.at[0], right), rcopy(r, r, ss, rs.at[0], left)]
            s.b += [rcopy(r0, r0, ss, rs.at[1], right), rcopy(r1, r1, ss, rs.at[1], left)]
    def start(s):
        for c in s.a: c.start()
    def relay(s):
        take_bytes(s.size(2, s.n), s.rs.at[0], s.h)
        for c in s.b: c.start()
    def finish(s):
        take_bytes(s.size(1, s.n), s.rs.at[1], s.h)

class Folds:
    def __init__(s, h, regs, phase, spans, r1, r2, ss, rs, take, size):
        s.h, s.ss, s.rs, s.size, s.n = h, ss, rs, size, sum(n for _, n in spans)
        s.r1, s.r2, s.take = r1, r2, take
        s.first, s.second, s.third, s.parts, s.items = [], [], [], [], []
        l, r = r2.at[0], r2.at[1]
        for g, (lo, n) in enumerate(spans):
            axis, reg = ORDERS[g][phase], regs[g]
            right, left = h.nbr(axis, 1), h.nbr(axis, 3)
            p0, p1 = halves(lo, n)
            R = lambda part, d: cut(reg(pl.ds(*part[:2]), h.at(axis, d)), part)
            T = lambda ref, part: cut(take(ref, pl.ds(*part[:2])), part)
            s.first += [rcopy(R(p0, 2), T(r1, p0), ss, rs.at[0], right), rcopy(R(p1, 2), T(r1, p1), ss, rs.at[0], left)]
            s.second += [rcopy(R(p1, 1), T(l, p1), ss, rs.at[1], right), rcopy(R(p0, 3), T(r, p0), ss, rs.at[1], left)]
            s.third += [rcopy(R(p0, 1), T(l, p0), ss, rs.at[1], right), rcopy(R(p1, 3), T(r, p1), ss, rs.at[1], left)]
            s.parts += [(p0, reg, h.at(axis, 1)), (p1, reg, h.at(axis, 3))]
            s.items.append((lo, n, reg, h.c[axis]))
    def start(s):
        for c in s.first + s.second: c.start()
    def add(s, part, reg, v):
        def one(k):
            ref, got = reg(k, v), s.take(s.r1, k)
            if part[2] is not None: ref, got = (x.at[pl.ds(112 * part[2], 112)] for x in (ref, got))
            ref[...] = (ref[...].astype(F32) + got[...].astype(F32)).astype(BF)
        if part[1] == 1: one(part[0])
        else: pl.loop(0, part[1])(lambda i: one(part[0] + i))
    def relay(s):
        take_bytes(s.size(1, s.n), s.rs.at[0], s.h)
        for p, c in zip(s.parts, s.third):
            s.add(*p); c.start()
    def total(s, k, reg, v):
        return reg(k, v)[...].astype(F32) + s.take(s.r2.at[0], k)[...].astype(F32) + s.take(s.r2.at[1], k)[...].astype(F32)
    def arrive(s): take_bytes(s.size(2, s.n), s.rs.at[1], s.h)

def take0(ref, k): return ref.at[k]
def take1(ref, k): return ref.at[:, k]

class Layer:
    def __init__(s, **kw): s.__dict__.update(kw)

    def reg3(s, g): return lambda sl, v: s.w.at[sl, v]
    def reg2(s, g): return lambda sl, v: s.pb.at[v, :, sl]
    def reg1(s, g): return lambda sl, v: s.pb.at[s.h.c[ORDERS[g][1]], v, sl]
    def span(s, g, k):
        if isinstance(k, int):
            return ATT[g] if k < 0 else (FFN[g], 1) if k == 0 else (FFN[g] + 2 * k - 1, 2)
        return FFN[g] + 2 * k - 1, 2
    def size3(s, m, n): return s.r1a.at[pl.ds(0, n)] if m == 1 else s.r2a.at[:, pl.ds(0, n)]
    def size2(s, m, n): return s.r1b.at[:, pl.ds(0, n)] if m == 1 else s.r2b.at[:, :, pl.ds(0, n)]
    def size1(s, m, n): return s.r1c.at[pl.ds(0, n)] if m == 1 else s.r2c.at[:, pl.ds(0, n)]
    def regs(s, p): return [(s.reg1, s.reg2, s.reg3)[p](g) for g in range(3)]
    def wave(s, waves, g, i): return ATT[g] if i == 0 else (FFN[g] + waves[i - 1][0], waves[i - 1][1])
    def spans(s, waves, i): return [s.wave(waves, g, i) for g in range(3)]
    def ring1(s, i): return Rings(s.h, s.regs(0), 0, s.spans(GATHER_WAVES, i), s.gss.at[0], s.grs.at[i], s.size1)
    def ring2(s, i): return Rings(s.h, s.regs(1), 1, s.spans(GATHER_WAVES, i), s.gss.at[1], s.grs.at[3 + i], s.size2)
    def ring3(s, k): return Rings(s.h, s.regs(2), 2, [s.span(g, k) for g in range(3)], s.gss.at[2], s.grs.at[7 + k], s.size3)
    def compact(s, k):
        for g in range(3):
            lo, n = s.span(g, k)
            c = s.h.c[ORDERS[g][2]]
            for i in range(0, n, 2):
                m = min(2, n - i)
                x = lanes([s.pb[:, :, lo + i + j].reshape(256, 128) for j in range(m)])
                y = nn(s.cmat[...], x).astype(BF)
                for j in range(m): s.w[lo + i + j, c] = y[:, 128 * j:128 * j + 128]
    def send3(s, k):
        s.compact(k)
        s.ring3(k).start()
    def relay3(s, k): s.ring3(k).relay()
    def finish3(s, k): s.ring3(k).finish()

    def fold3(s, k):
        return Folds(s.h, s.regs(2), 2, [s.span(g, k) for g in range(3)], s.r1a, s.r2a, s.fss.at[2], s.frs.at[k + 1], take0, s.size3)
    def fold2(s, i): return Folds(s.h, s.regs(1), 1, s.spans(SUM_WAVES, i), s.r1b, s.r2b, s.fss.at[1], s.frs.at[11 + i], take1, s.size2)
    def fold1(s, i): return Folds(s.h, s.regs(0), 0, s.spans(SUM_WAVES, i), s.r1c, s.r2c, s.fss.at[0], s.frs.at[15 + i], take0, s.size1)
    def fold_start(s, k): s.fold3(k).start()
    def fold_relay(s, k): s.fold3(k).relay()
    def fold_expand(s, k):
        f = s.fold3(k)
        f.arrive()
        for lo, n, reg, v in f.items:
            for i in range(0, n, 2):
                m = min(2, n - i)
                x = lanes([f.total(lo + i + j, reg, v).astype(BF) for j in range(m)])
                y = nn(s.emat[...], x).astype(BF)
                for j in range(m): s.pb[:, :, lo + i + j] = y[:, 128 * j:128 * j + 128].reshape(4, 4, 16, 128)
    def settle2(s, f):
        f.arrive()
        for lo, n, reg, v in f.items:
            @pl.loop(0, n)
            def _(i): s.pb[v, :, lo + i] = f.total(lo + i, reg, v).astype(BF)
    def settle1(s, f):
        f.arrive()
        for lo, n, reg, v in f.items:
            @pl.loop(0, n)
            def _(i): s.grads[lo + i] = f.total(lo + i, reg, v)
    def sent(s, sems):
        for ref, i in ((s.pb.at[0, pl.ds(0, 3)], 0), (s.pb.at[pl.ds(0, 3)], 1), (s.w.at[:, pl.ds(0, 3)], 2)):
            take_bytes(ref, sems.at[i], s.h)

    def small(s, t, p):
        a = AX[p]
        own = s.slots.at[t, p, s.h.c[a]]
        return [rcopy(own, own, s.sss.at[0], s.srs.at[t, p], s.h.nbr(a, d)) for d in (1, 2, 3)]
    def small_start(s, t, p, v):
        s.slots[t, p, s.h.c[AX[p]]] = v
        for c in s.small(t, p): c.start()
    def small_end(s, t, p):
        q = s.slots.at[t, p]
        take_bytes(q.at[pl.ds(0, 3)], s.srs.at[t, p], s.h)
        return (q[0] + q[1]) + (q[2] + q[3])

    def slab(s, k): return s.w[k].reshape(W, 128)
    def codes(s, lo, n): return lanes([s.slab(lo + i) for i in range(n)])
    def pair(s, k, lo, n):
        d = pl.ds(lo, n)
        return rcopy(s.xs.at[d], s.xr.at[k % 2, d], s.xss.at[k, lo // 128], s.xrs.at[k, lo // 128], (s.h.dp, 1 - s.h.mp))
    def offer(s, k, part, lo=0):
        s.xs[pl.ds(lo, part.shape[0])] = part.astype(BF)
        s.pair(k, lo, part.shape[0]).start()
    def accept(s, k, n, lo=0):
        s.pair(k, lo, n).wait()
        return s.xs[pl.ds(lo, n)].astype(F32) + s.xr[k % 2, pl.ds(lo, n)].astype(F32)
    def exchange(s, k, part):
        s.offer(k, part)
        return s.accept(k, part.shape[0])

    def own_block(s):
        att = lanes([r[...] for r in (s.q_codes, s.k_codes, s.v_codes, s.o_codes)])
        for base, x in ((0, att), (FFN[0], s.g_codes[...]), (FFN[1], s.u_codes[...]), (FFN[2], s.d_codes[...])):
            x = rows([x, jnp.zeros((2, x.shape[1]), BF)])
            for i in range(x.shape[1] // 128):
                k = base + i
                g = next(g for g in range(3) if ATT[g][0] <= k < sum(ATT[g]) or FFN[g] <= k < FFN[g] + 19)
                s.pb[s.h.c[ORDERS[g][1]], s.h.c[ORDERS[g][0]], k] = x[:, 128 * i:128 * i + 128]

    def matrices(s):
        i, j = iota((224, 256), 0), iota((224, 256), 1)
        s.cmat[...] = jnp.where(j == i + 2 * lax.shift_right_logical(i * 4682, 16), 1.0, 0.0).astype(BF)
        i, j = iota((256, 224), 1), iota((256, 224), 0)
        s.emat[...] = jnp.where(j == i + 2 * lax.shift_right_logical(i * 4682, 16), 1.0, 0.0).astype(BF)

    def row(s, r): return r[...].reshape(1, r.shape[0])

    def prologue(s):
        i = iota((W, 1), 0)
        blk = lax.shift_right_logical(i * 4682, 16)
        r = i - 14 * blk
        c = {"x": lax.shift_right_logical(blk, 4), "y": jnp.bitwise_and(lax.shift_right_logical(blk, 2), 3), "z": jnp.bitwise_and(blk, 3)}
        j = iota((W, W), 1)
        for g in range(2):
            a1, a2, a3 = (c[a] for a in ORDERS[g])
            s.q[g] = jnp.where(j == ((a3 * 4 + a2) * 4 + a1) * 14 + r, 1.0, 0.0).astype(BF)
        l0, l1 = s.lengths[0, 0], s.lengths[0, 1]
        def seg_of(i): return jnp.where(i >= l0, 1, 0) + jnp.where(i >= l0 + l1, 1, 0)
        ti, tj = iota((128, 128), 0), iota((128, 128), 1)
        si, sj = seg_of(ti), seg_of(tj)
        s.allow[...] = jnp.where((si == sj) & (tj <= ti), 1.0, 0.0)
        pos = ti - jnp.where(si == 0, 0, jnp.where(si == 1, l0, l0 + l1))
        lane = jnp.bitwise_and(tj, 31).astype(F32)
        ang = pos.astype(F32) * jnp.exp(lane * (-math.log(10000.0) / 32))
        co, sn = jnp.cos(ang), jnp.sin(ang)
        sn = jnp.where(jnp.bitwise_and(tj, 63) < 32, -sn, sn)
        s.cos[...] = co
        s.sin[...] = sn
        x = s.hidden[...].astype(F32)
        nrm = (x * rinv(x) * s.gains[0:1]).astype(BF)
        s.nrm[2] = nrm
        for g in range(2): s.nrm[g] = nn(nrm, s.q[g]).astype(BF)
        s.qkvs[...] = jnp.zeros_like(s.qkvs)
        s.qkvs[:, 0:576] = lanes([s.row(r) for r in (s.q_scale, s.k_scale, s.v_scale)])
        for to, r in ((s.osc, s.o_scale), (s.gsc, s.g_scale), (s.usc, s.u_scale), (s.dsc, s.d_scale)): to[...] = s.row(r)

    def swap(s, v):
        lane = jnp.bitwise_and(iota((128, 512), 1), 63)
        return jnp.where(lane < 32, pltpu.roll(v, 512 - 32, 1), pltpu.roll(v, 32, 1))

    def probs(s, qs, k):
        th = jnp.tanh(nt(qs, k) * (0.125 / CAP))
        e = jnp.exp(CAP * th) * rows([s.allow[...]] * 7)
        return th, e / jnp.sum(e, axis=-1, keepdims=True)

    def heads(s, qk): return rows([qk[:, 64 * i:64 * i + 64] for i in range(7)]), qk[:, 448:512]

    def attention(s, b):
        rs = rsum(s.nrm[2])
        lin = lanes([nn(s.nrm[0], units(s.codes(0, 2), b)), nn(s.nrm[1], units(s.codes(2, 2), b)), nn(s.nrm[2], units(s.codes(4, 1), b))])
        lin = (lin * MUL[b] + OFF[b] * rs) * s.qkvs[...]
        s.lin[b] = lin.astype(s.lin.dtype)
        qk = lin[:, :512]
        qk = (qk * lanes([s.cos[...]] * 4) + s.swap(qk) * lanes([s.sin[...]] * 4)).astype(BF)
        qs, k = s.heads(qk)
        v = lin[:, 512:576].astype(BF)
        s.qk[b], s.v[b] = qk, v
        _, pr = s.probs(qs, k)
        mx = nn(pr.astype(BF), v).astype(BF)
        mixed = lanes([jnp.zeros((128, 64), BF)] + [mx[128 * i:128 * i + 128] for i in range(7)])
        d = pl.ds(128 * b, 128)
        s.mixed[d] = mixed
        s.acc[0, d] = nt(mixed, units(s.codes(4, 4), b)) * MUL[b] + OFF[b] * rsum(mixed)

    def lifted(s, b):
        br = s.bu[pl.ds(128 * b, 128)] * s.osc[...]
        r = rinv(br)
        return s.hidden[...].astype(F32) + br * r * s.gains[1:2], br, r

    def middle(s):
        s.bu[...] = s.exchange(0, s.acc[0])
        for b in range(3):
            d = pl.ds(128 * b, 128)
            lif = s.lifted(b)[0]
            n2 = (lif * rinv(lif) * s.gains[2:3]).astype(BF)
            s.rsn[d] = jnp.broadcast_to(rsum(n2), (128, 128))
            for g in range(2): s.n2[g, d] = nn(n2, s.q[g]).astype(BF)
        for g in range(2): s.n2t[g] = s.n2[g].T
        s.acc[0] = jnp.zeros((384, W), F32)
        s.asum[...] = jnp.zeros_like(s.asum)

    def srow(s, ref, k, n): return ref[:, pl.ds(128 * k if isinstance(k, int) else pl.multiple_of(k * 128, 128), n * 128)]

    def ffn_fwd(s, k, n, last=False):
        wg, wu, wd = (s.codes(f + k, n) for f in FFN)
        sg, su = s.srow(s.gsc, k, n), s.srow(s.usc, k, n)
        for b in range(3):
            d = pl.ds(128 * b, 128)
            rs = s.rsn[d][:, 0:1] * OFF[b]
            g = (nn(s.n2[0, d], units(wg, b)) * MUL[b] + rs) * sg
            u = (nn(s.n2[1, d], units(wu, b)) * MUL[b] + rs) * su
            act = (0.5 * g * (1.0 + jnp.tanh(C0 * (g + C1 * g * g * g))) * u).astype(BF)
            for i in range(n):
                c = slice(128 * i, 128 * i + 128)
                s.g[k + i, d], s.u[k + i, d] = g[:, c].astype(BF), u[:, c].astype(BF)
            s.acc[0, d] += nt(act, units(wd, b))
            s.asum[0, d] += jnp.broadcast_to(rsum(act) * OFF[b], (128, 128))
            if last: s.offer(1, s.acc[0, d] * MUL[b] + s.asum[0, d][:, 0:1], 128 * b)

    def scaled(s, g):
        return rows([s.acc[g, pl.ds(128 * b, 128)] * MUL[b] for b in range(3)]) + s.asum[g][:, 0:1]

    def turn(s):
        dgain, dsd = 0.0, 0.0
        for b in range(3):
            d = pl.ds(128 * b, 128)
            f = s.accept(1, 128, 128 * b)
            feed = f * s.dsc[...]
            r = rinv(feed)
            s.result[b] = (s.lifted(b)[0] + feed * r * s.gains[3:4]).astype(BF)
            df, dg = rms_back(feed, r, s.gains[3:4], s.cot[b].astype(F32))
            dgain += dg
            dfl = df.astype(BF)
            dsd += csum(dfl.astype(F32) * f)
            s.n2[0, d] = dfl
            dfs = (df * s.dsc[...]).astype(BF)
            s.n2[1, d] = dfs
            s.rsn[d] = jnp.broadcast_to(rsum(dfs) * OFF[b], (128, 128))
        s.sm[11:12] = dgain
        s.sm[7:8] = dsd
        s.dft[...] = s.n2[0].T
        s.acc[...] = jnp.zeros_like(s.acc)
        s.asum[...] = jnp.zeros_like(s.asum)

    def ffn_dx(s, k, n):
        wg, wu, wd = (s.codes(f + k, n) for f in FFN)
        sg, su = s.srow(s.gsc, k, n), s.srow(s.usc, k, n)
        al = []
        gsum, usum = 0.0, 0.0
        get = lambda ref, d: lanes([ref[k + i, d] for i in range(n)])
        for b in range(3):
            d = pl.ds(128 * b, 128)
            da = nn(s.n2[1, d], units(wd, b)) * MUL[b] + s.rsn[d][:, 0:1]
            g, u = get(s.g, d).astype(F32), get(s.u, d).astype(F32)
            t = jnp.tanh(C0 * (g + C1 * g * g * g))
            hp = 0.5 * (1.0 + t)
            gelu = g * hp
            du = da * gelu
            dg = da * u * (hp + 0.5 * g * (1.0 - t * t) * C0 * (1.0 + 3 * C1 * g * g))
            dgl, dul = dg.astype(BF), du.astype(BF)
            al.append((gelu * u).astype(BF))
            for i in range(n):
                c = slice(128 * i, 128 * i + 128)
                s.g[k + i, d], s.u[k + i, d] = dgl[:, c], dul[:, c]
            gsum += csum(dgl.astype(F32) * g); usum += csum(dul.astype(F32) * u)
            dgs, dus = (dg * sg).astype(BF), (du * su).astype(BF)
            s.acc[0, d] += nt(dgs, units(wg, b))
            s.acc[1, d] += nt(dus, units(wu, b))
            s.asum[0, d] += jnp.broadcast_to(rsum(dgs) * OFF[b], (128, 128))
            s.asum[1, d] += jnp.broadcast_to(rsum(dus) * OFF[b], (128, 128))
        at = lambda ref: ref.at[:, pl.ds(128 * k if isinstance(k, int) else pl.multiple_of(k * 128, 128), n * 128)]
        at(s.gsg)[...] = gsum / sg
        at(s.usg)[...] = usum / su
        s.put(2, k, n, nn(s.dft[...], rows(al)))

    def put(s, g, k, n, dw):
        dw = dw.astype(BF)
        for i in range(n): s.w[FFN[g] + k + i] = dw[:, 128 * i:128 * i + 128].reshape(4, 224, 128)
    def ffn_dw(s, k, n):
        for g, ref in enumerate((s.g, s.u)): s.put(g, k, n, nn(s.n2t[g], lanes([ref[k + i] for i in range(n)])))

    def pack(s):
        for i in range(3):
            m = min(W, 2432 - W * i)
            s.sm[i:i + 1, 0:m] = s.gsg[:, W * i:W * i + m]
            s.sm[3 + i:4 + i, 0:m] = s.usg[:, W * i:W * i + m]

    def lower(s):
        s.offer(2, sum(nt(s.scaled(g).astype(BF), s.q[g]) for g in range(2)))
        s.fill()
        dn = s.accept(2, 384)
        dg1, dg2, dso, din = 0.0, 0.0, 0.0, 0.0
        for b in range(3):
            d = pl.ds(128 * b, 128)
            lif, br, r = s.lifted(b)
            dl, dg = rms_back(lif, rinv(lif), s.gains[2:3], dn[128 * b:128 * b + 128])
            dg2 += dg
            dl = dl + s.cot[b].astype(F32)
            din = din + dl
            db, dg = rms_back(br, r, s.gains[1:2], dl)
            dg1 += dg
            dbl = db.astype(BF)
            dso += csum(dbl.astype(F32) * s.bu[d])
            s.n2[0, d] = dbl
            s.n2[1, d] = (db * s.osc[...]).astype(BF)
        s.acc[1, pl.ds(0, 128)] = din
        s.sm[9:10], s.sm[10:11], s.sm[6:7] = dg1, dg2, dso

    def attention_back(s, b):
        d = pl.ds(128 * b, 128)
        dbs = s.n2[1, d]
        dm = (nn(dbs, units(s.codes(4, 4), b)) * MUL[b] + OFF[b] * rsum(dbs)).astype(BF)
        dms = rows([dm[:, 64 * i + 64:64 * i + 128] for i in range(7)])
        v = s.v[b]
        qs, k = s.heads(s.qk[b])
        th, pr = s.probs(qs, k)
        dp = nt(dms, v)
        gv = tn(pr.astype(BF), dms)
        dc = pr * (dp - jnp.sum(dp * pr, axis=-1, keepdims=True))
        dr = (dc * (1.0 - th * th)).astype(BF)
        gq = nn(dr, k) * 0.125
        gk = tn(dr, qs) * 0.125
        gqk = lanes([gq[128 * i:128 * i + 128] for i in range(7)] + [gk])
        gqk = gqk * lanes([s.cos[...]] * 4) - s.swap(gqk) * lanes([s.sin[...]] * 4)
        g = lanes([gqk, gv, jnp.zeros((128, 64), F32)])
        gl = g.astype(BF).astype(F32)
        gs = (g * s.qkvs[...]).astype(BF)
        sg = csum(gl * s.lin[b].astype(F32))
        for i, (c, lo, n) in enumerate(((slice(0, 256), 0, 2), (slice(256, 512), 2, 2), (slice(512, 640), 4, 1))):
            part = nt(gs[:, c], units(s.codes(lo, n), b)) * MUL[b] + rsum(gs[:, c]) * OFF[b]
            e = pl.ds(128 * i, 128)
            if b: s.acc[0, e] += part
            else: s.acc[0, e] = part
        if b:
            s.acc[1, pl.ds(128, 128), 0:640] += gl; s.sqk[...] += sg
        else:
            s.acc[1, pl.ds(128, 128), 0:640] = gl; s.sqk[...] = sg

    def attention_grads(s):
        sc = s.qkvs[...]
        s.sm[12:13, 0:640] = jnp.where(sc > 0, s.sqk[...] / sc, 0.0)
        dqk = s.acc[1, pl.ds(128, 128), 0:640].astype(BF)
        dw = [nn(s.nrm[0].T, dqk[:, 0:256]), nn(s.nrm[1].T, dqk[:, 256:512])]
        lhs = lanes([s.nrm[2].T, s.n2[0].T])
        rhs = rows([lanes([dqk[:, 512:576], jnp.zeros((128, 448), BF)]), s.mixed[...]])
        dw.append(nn(lhs, rhs))
        for (lo, n), x in zip(ATT, dw):
            x = x.astype(BF)
            for i in range(n): s.w[lo + i] = x[:, 128 * i:128 * i + 128].reshape(4, 224, 128)

    def last_offer(s):
        s.offer(3, sum(nt(s.acc[0, pl.ds(128 * g, 128)].astype(BF), s.q[g]) for g in range(2)) + s.acc[0, pl.ds(256, 128)])
    def last(s):
        dn = s.accept(3, 128)
        x = s.hidden[...].astype(F32)
        dx, dg = rms_back(x, rinv(x), s.gains[0:1], dn)
        s.sm[8:9] = dg
        s.in_grad[...] = (s.acc[1, pl.ds(0, 128)] + dx).astype(BF)

LOADS = ("hidden", "cot", "lengths", "gains", "q_scale", "k_scale", "v_scale", "o_scale", "g_scale", "u_scale", "d_scale")
STORES = ("grads", "smo", "result", "in_grad")
CODES = ("q_codes", "k_codes", "v_codes", "o_codes", "g_codes", "u_codes", "d_codes")
INS = CODES + tuple(n + "_in" for n in LOADS)
OUTS = tuple(n + "_out" for n in STORES)
def scratch():
    V, D = pltpu.VMEM, pltpu.SemaphoreType.DMA
    return dict(
        hidden=V((128, W), BF), cot=V((3, 128, W), BF), lengths=pltpu.SMEM((1, 3), jnp.int32), gains=V((4, W), F32),
        q_scale=V((448,), F32), k_scale=V((64,), F32), v_scale=V((64,), F32), o_scale=V((W,), F32), g_scale=V((2432,), F32),
        u_scale=V((2432,), F32), d_scale=V((W,), F32), grads=V((65, 16, 128), F32), smo=V((16, W), F32), result=V((3, 128, W), BF),
        in_grad=V((128, W), BF), isem=D((len(LOADS),)), osem=D((len(STORES) + 2,)),
        w=V((65, 4, 224, 128), BF), pb=V((4, 4, 65, 16, 128), BF),
        r1a=V((65, 224, 128), BF), r2a=V((2, 65, 224, 128), BF), r1b=V((4, 65, 16, 128), BF), r2b=V((2, 4, 65, 16, 128), BF),
        r1c=V((65, 16, 128), BF), r2c=V((2, 65, 16, 128), BF), slots=V((2, 3, 4, 8, W), F32), sm=V((16, W), F32),
        cmat=V((224, 256), BF), emat=V((256, 224), BF), q=V((2, W, W), BF), allow=V((128, 128), F32), cos=V((128, 128), F32),
        sin=V((128, 128), F32), nrm=V((3, 128, W), BF), qkvs=V((1, 640), F32), lin=V((3, 128, 640), BF), qk=V((3, 128, 512), BF),
        v=V((3, 128, 64), BF), mixed=V((384, 512), BF), acc=V((2, 384, W), F32), bu=V((384, W), F32),
        n2=V((2, 384, W), BF), n2t=V((2, W, 384), BF), rsn=V((384, 128), F32), asum=V((2, 384, 128), F32),
        g=V((19, 384, 128), BF), u=V((19, 384, 128), BF), dft=V((W, 384), BF),
        gsg=V((1, 2432), F32), usg=V((1, 2432), F32),
        sqk=V((1, 640), F32), osc=V((1, W), F32), dsc=V((1, W), F32), gsc=V((1, 2432), F32), usc=V((1, 2432), F32), xs=V((384, W), BF), xr=V((2, 384, W), BF), xss=D((4, 3)), xrs=D((4, 3)),
        gss=D((3,)), grs=D((17, 2)), fss=D((3,)), frs=D((19, 2)), sss=D((1,)), srs=D((2, 3)),)

def body(names, *refs):
    h = Here()
    s = Layer(h=h, **dict(zip(names, refs)))
    loads = [pltpu.make_async_copy(getattr(s, n + "_in"), getattr(s, n), s.isem.at[i]) for i, n in enumerate(LOADS)]
    stores = []
    def store(i, n, part=None):
        a, b = getattr(s, n), getattr(s, n + "_out")
        if part is not None: a, b = a.at[pl.ds(*part)], b.at[pl.ds(*part)]
        stores.append(pltpu.make_async_copy(a, b, s.osem.at[i]))
        stores[-1].start()
    for c in loads: c.start()
    bar = pltpu.get_barrier_semaphore()
    for a in AX:
        for d in (1, 2, 3):
            pl.semaphore_signal(bar, inc=1, device_id=h.nbr(a, d), device_id_type=MESH)
    pl.semaphore_signal(bar, inc=1, device_id=(h.dp, 1 - h.mp), device_id_type=MESH)
    s.own_block()
    pl.semaphore_wait(bar, 10)
    one, two = [s.ring1(i) for i in range(3)], [s.ring2(i) for i in range(3)]
    def do(what, r): getattr(r, what)()
    for i in range(3): do("start", one[i])
    s.matrices()
    do("relay", one[0])
    do("relay", one[1])
    do("finish", one[0])
    do("start", two[0])
    do("relay", one[2])
    do("finish", one[1])
    do("start", two[1])
    s.sm[...] = jnp.zeros_like(s.sm)
    do("relay", two[0])
    do("finish", one[2])
    do("start", two[2])
    for c in loads: c.wait()
    s.prologue()
    do("finish", two[0])
    s.send3(-1)
    do("relay", two[1])
    do("finish", two[1])
    s.send3(0); s.send3(1)
    s.relay3(-1)
    do("relay", two[2])
    s.send3(2)
    s.finish3(-1)
    s.attention(0)
    s.relay3(0); s.send3(3)
    do("finish", two[2])
    s.attention(1)
    s.relay3(1); s.send3(4)
    s.attention(2)
    s.relay3(2); s.send3(5)
    s.middle()
    s.relay3(3); s.send3(6)
    s.finish3(0)
    s.ffn_fwd(0, 1)
    @pl.loop(1, NCH - 1)
    def _(k):
        @pl.when(k < NCH - 3)
        def _(): s.relay3(k + 3)
        @pl.when(k < NCH - 6)
        def _(): s.send3(k + 6)
        s.finish3(k)
        s.ffn_fwd(2 * k - 1, 2)
    s.finish3(NCH - 1)
    s.ffn_fwd(17, 2, last=True)
    s.turn()
    store(2, "result")
    s.sent(s.gss)
    def emit(k):
        s.ffn_dw(2 * k - 1, 2)
        s.fold_start(k)
    s.ffn_dx(0, 1)
    s.ffn_dw(0, 1)
    s.fold_start(0)
    @pl.loop(1, 7)
    def _(k):
        s.ffn_dx(2 * k - 1, 2)
        emit(k)
        @pl.when(k == 2)
        def _(): s.fold_relay(0)
        @pl.when(k > 2)
        def _(): s.fold_relay(k - 2)
    @pl.loop(7, NCH)
    def _(k):
        s.ffn_dx(2 * k - 1, 2)
        @pl.when(k < 9)
        def _(): s.fold_relay(k - 2)
    s.pack()
    s.fill = lambda: emit(7)
    s.lower()
    s.small_start(0, 0, s.sm[0:8])
    f2, f1 = [s.fold2(i) for i in range(4)], [s.fold1(i) for i in range(4)]
    s.fold_expand(0)
    @pl.loop(1, 4)
    def _(k): s.fold_expand(k)
    do("start", f2[1])
    s.attention_back(0)
    emit(8)
    s.attention_back(1)
    s.fold_relay(7)
    emit(9)
    do("relay", f2[1])
    s.attention_back(2)
    s.attention_grads()
    s.fold_start(-1)
    s.last_offer()
    @pl.loop(4, 7)
    def _(k): s.fold_expand(k)
    do("start", f2[2])
    s.fold_relay(8)
    s.fold_relay(9)
    s.last()
    store(3, "in_grad")
    s.small_start(1, 0, s.sm[8:16])
    s.small_start(0, 1, s.small_end(0, 0))
    s.settle2(f2[1])
    do("start", f1[1])
    s.fold_relay(-1)
    do("relay", f2[2])
    @pl.loop(7, NCH)
    def _(k): s.fold_expand(k)
    do("start", f2[3])
    s.fold_expand(-1)
    do("start", f2[0])
    do("relay", f1[1])
    s.settle2(f2[2])
    do("start", f1[2])
    s.small_start(0, 2, s.small_end(0, 1))
    do("relay", f2[3])
    do("relay", f2[0])
    s.small_start(1, 1, s.small_end(1, 0))
    s.settle1(f1[1])
    do("relay", f1[2])
    s.settle2(f2[3])
    do("start", f1[3])
    s.settle2(f2[0])
    do("start", f1[0])
    s.small_start(1, 2, s.small_end(1, 1))
    s.settle1(f1[2])
    do("relay", f1[3])
    do("relay", f1[0])
    s.settle1(f1[3])
    s.settle1(f1[0])
    s.smo[0:8] = s.small_end(0, 2)
    s.smo[8:16] = s.small_end(1, 2)
    store(1, "smo")
    store(0, "grads")
    s.sent(s.fss)
    for c in stores: c.wait()
    take_bytes(s.slots.at[:, :, pl.ds(0, 3)], s.sss.at[0], s.h)

def layer(*ins):
    A = pl.BlockSpec(memory_space=pl.ANY)
    sc = scratch()
    return pl.pallas_call(
        functools.partial(body, INS + OUTS + tuple(sc)),
        out_shape=(jax.ShapeDtypeStruct((65, 16, 128), F32), jax.ShapeDtypeStruct((16, W), F32), jax.ShapeDtypeStruct((3, 128, W), BF),
                   jax.ShapeDtypeStruct((128, W), BF)),
        in_specs=[pl.BlockSpec(memory_space=pltpu.VMEM)] * len(CODES) + [A] * len(LOADS), out_specs=(A,) * 4, scratch_shapes=list(sc.values()),
        compiler_params=pltpu.CompilerParams(collective_id=0, has_side_effects=True, vmem_limit_bytes=63 << 20),
    )(*ins)

SHAPES = [(14, 448), (14, 64), (14, 64), (14, 448), (14, 2432), (14, 2432), (14, 2432), (448,), (64,), (64,), (896,), (2432,), (2432,), (896,), (4, 896)]

def unpack_body(*refs):
    ins, outs, own, (g_ref, sm_ref, isem, osem) = refs[:4], refs[4:21], refs[21:38], refs[38:]
    cs = [pltpu.make_async_copy(x, y, isem.at[i]) for i, (x, y) in enumerate(zip(ins, (g_ref, sm_ref) + own[:2]))]
    out = [pltpu.make_async_copy(x, y, osem.at[i]) for i, (x, y) in enumerate(zip(own, outs))]
    for c in cs: c.start()
    (q, k, v, o, gate, up, down), vecs, gains = own[2:9], own[9:16], own[16]
    for i in range(2):
        cs[2 + i].wait(); out[i].start()
    for i in range(2): cs[i].wait()
    cat = lambda lo, n: lanes([g_ref[i] for i in range(lo, lo + n)])[:14]
    for i, (ref, f) in enumerate(zip((gate, up, down), FFN)):
        ref[...] = cat(f, 19)
        out[6 + i].start()
    att = cat(0, 8)
    q[...], k[...], v[...], o[...] = att[:, :448], att[:, 448:512], att[:, 512:576], att[:, 576:]
    for i in range(2, 6): out[i].start()
    long = lambda r: lanes([sm_ref[r:r + 1], sm_ref[r + 1:r + 2], sm_ref[r + 2:r + 3, 0:640]])
    parts = (sm_ref[12:13, 0:448], sm_ref[12:13, 448:512], sm_ref[12:13, 512:576], sm_ref[6:7], long(0), long(3), sm_ref[7:8])
    for ref, row in zip(vecs, parts): ref[...] = row.reshape(ref.shape[0])
    gains[...] = sm_ref[8:12]
    for c in out[9:]: c.start()
    for c in out: c.wait()

def unpack(*a):
    A, V, D = pl.BlockSpec(memory_space=pl.ANY), pltpu.VMEM, pltpu.SemaphoreType.DMA
    outs = [jax.ShapeDtypeStruct(x.shape, BF) for x in a[2:]] + [jax.ShapeDtypeStruct(x, F32) for x in SHAPES]
    return pl.pallas_call(unpack_body, out_shape=outs, in_specs=[A] * 4, out_specs=[A] * len(outs),
                          scratch_shapes=[V(x.shape, x.dtype) for x in outs] + [V((65, 16, 128), F32), V((16, W), F32), D((4,)), D((17,))],
                          compiler_params=pltpu.CompilerParams(vmem_limit_bytes=63 << 20))(*a)

def local(hidden_in, cotangent, lengths, gains, query_codes, key_codes, value_codes, output_codes, gate_codes, upward_codes, down_codes,
          query_scale, key_scale, value_scale, output_scale, gate_scale, upward_scale, down_scale):
    out = layer(query_codes, key_codes, value_codes, output_codes.T, gate_codes, upward_codes, down_codes.T, hidden_in, cotangent, lengths, gains,
                query_scale, key_scale, value_scale, output_scale, gate_scale, upward_scale, down_scale)
    out = unpack(*out)
    return (*out[:5], out[5].T, *out[6:8], out[8].T, *out[9:])

def solution(mesh):
    d, c, r = P("dp", None), P("dp", "mp"), P("mp", "dp")
    return jax.shard_map(local, mesh=mesh,
        in_specs=(d, P(None, "dp", None), d, P(), c, c, c, r, c, c, r, P("mp"), P("mp"), P("mp"), P(), P("mp"), P("mp"), P()),
        out_specs=(P(None, "dp", None), d, c, c, c, r, c, c, r, P("mp"), P("mp"), P("mp"), P(), P("mp"), P("mp"), P(), P()),
        check_vma=False)
```
